256 devices in a mesh: band: 16 (over x_lo, z), dom: 16 (over y, x_hi, core).
Axes of the slice: x: 4 (x_hi: 2, x_lo: 2; x = x_hi * 2 + x_lo), y: 4, z: 8, core: 2. Of those that a mesh axis runs over, the one named last changes fastest.
Arguments:
- orbitals: float32 [64, 96, 32, 128], P('band', 'dom'), may hold values from -6 to 6
- potential: float32 [96, 32, 128], P('dom'), may hold values from -1.5 to 1.5
- support: int32 [16, 2, 48, 384], P('dom'), may hold values from 0 to 24575
- projectors: float32 [16, 2, 48, 8, 384], P('dom'), may hold values from -0.4375 to 0.4375
- slot_rows: int32 [16, 2, 48], P('dom'), may hold values from 0 to 47, each once within a row
- energies: float32 [16, 48, 8], replicated, may hold values from -3 to 3
- panel_orbitals: bfloat16 [512, 96, 32, 128], P('band', 'dom'), may hold values from -6 to 6
Outputs:
- filtered: float32 [64, 96, 32, 128], P('band', 'dom')
- correlation: float32 [64, 512], P('dom', 'band')
The draws below stay inside these ranges and needn't reach their ends.
Inputs may be any that keep to these rules, and one draw needn't show every extreme that they name: `support`: cell numbers within the block; a cell may repeat. `slot_rows`: on each block, the home slots (index 0) name every atom row once, and so do the spilled slots (index 1); spilled slots of block b belong to atoms homed on block b - 1, cyclically.
All inputs are finite; a program needn't handle non-finite values.
Results may differ from the reference program's by a relative error of at most 0.0029.
Values may be sent and summed in bfloat16 or wider, within the bound.
A program may use at most 128 MiB of HBM per device.

```python
import math
import jax
import jax.numpy as jnp
from jax import lax

CX = 6
CY = 32
CZ = 128
ATOM_DEV = 48
SUPP = 384
NPA = 8
BLOCKS = 16
NX = 96
WINDOW = 64
PANEL = 512
N_DOM = 16


def touch_ends(entries, own_key, low, largest):
    spot = [jax.random.randint(jax.random.fold_in(own_key, axis), (), 0, length) for axis, length in enumerate(entries.shape)]
    widest = entries.shape.index(max(entries.shape))
    neighbour = spot[:widest] + [(spot[widest] + 1) % entries.shape[widest]] + spot[widest + 1:]
    return entries.at[tuple(spot)].set(low).at[tuple(neighbour)].set(largest)


def block_levels(key, dims, cuts, low, top_value):
    def one(dim, shards_of):
        steps = jax.random.uniform(jax.random.fold_in(jax.random.fold_in(key, 6), dim), (shards_of,), jnp.float32, low / len(cuts), top_value / len(cuts))
        return jnp.repeat(jnp.exp(steps), dims[dim] // shards_of).reshape((-1,) + (1,) * (len(dims) - dim - 1))

    loudness = one(*cuts[0])
    for cut in cuts[1:]:
        loudness = loudness * one(*cut)
    return loudness


def centred(key, extent, deviation, bound, split=(), kind=jnp.bfloat16):
    factor_of = block_levels(key, extent, split, -0.22, 0.18) if split else 1.0
    array = jax.random.normal(key, extent, jnp.float32) * deviation * factor_of
    return jnp.minimum(jnp.maximum(array, -bound), bound).astype(kind)


def setup_inputs(seed: int = 0) -> dict:
    seeds = jax.random.split(jax.random.key(seed), 8)
    orbitals = centred(seeds[0], (WINDOW, NX, CY, CZ), 1.0, 6.0, ((0, 16), (1, 16)), jnp.float32)
    potential = jnp.clip(jax.random.uniform(seeds[1], (NX, CY, CZ), jnp.float32, -1.5, 1.5) * block_levels(seeds[1], (NX, CY, CZ), ((0, 16),), -0.4, 0.0), -1.5, 1.5)
    support = touch_ends(jax.random.randint(seeds[2], (BLOCKS, 2, ATOM_DEV, SUPP), 0, CX * CY * CZ), jax.random.fold_in(seeds[2], 1), 0, (CX * CY * CZ) - 1).astype(jnp.int32)
    projectors = centred(seeds[3], (BLOCKS, 2, ATOM_DEV, NPA, SUPP), (SUPP // 2) ** -0.5, 0.4375, ((0, 16),), jnp.float32)
    slot_rows = jax.vmap(lambda own: jax.random.permutation(own, ATOM_DEV))(jax.random.split(seeds[4], BLOCKS * 2)).reshape((BLOCKS, 2, ATOM_DEV)).astype(jnp.int32)
    energies = jnp.clip(jax.random.uniform(seeds[5], (BLOCKS, ATOM_DEV, NPA), jnp.float32, -3.0, 3.0), -3.0, 3.0)
    panel_orbitals = centred(seeds[6], (PANEL, NX, CY, CZ), 1.0, 6.0, ((0, 16), (1, 16)))
    return {"orbitals": orbitals, "potential": potential, "support": support, "projectors": projectors, "slot_rows": slot_rows, "energies": energies, "panel_orbitals": panel_orbitals}


def tapered_stencil():
    unscaled = [2.0 * (-1.0) ** (reach + 1) * math.sin(math.pi * reach / 8.0) / (math.pi * reach / 8.0 * reach * reach) for reach in range(1, 7)]
    moment = sum(reach * reach * unscaled[reach - 1] for reach in range(1, 7))
    side_terms = [neighbour_term / moment for neighbour_term in unscaled]
    return tuple([-2.0 * sum(side_terms)] + side_terms)


center_shift = 7.5
half_width = 6.5


def kinetic(functions):
    stencil = tapered_stencil()
    summed = 3.0 * stencil[0] * functions
    for reach in range(1, 7):
        for along in (1, 2, 3):
            summed = summed + stencil[reach] * (jnp.roll(functions, reach, along) + jnp.roll(functions, -reach, along))
    return -0.5 * summed


def nonlocal_term(functions, support, projectors, slot_rows, energies):
    orbital_count = functions.shape[0]
    cell_count = CX * CY * CZ
    blocked = functions.reshape(orbital_count, N_DOM, cell_count).transpose(1, 0, 2)

    def project(flattened, footprint, values):
        sampled = flattened[:, footprint]
        return jnp.einsum("sajq,osaq->sajo", values, sampled, precision=lax.Precision.HIGHEST)

    partials = jax.vmap(project)(blocked, support, projectors)

    def place_rows(piece, rows):
        return jnp.zeros_like(piece).at[rows].set(piece)

    home_table = jax.vmap(place_rows)(partials[:, 0], slot_rows[:, 0])
    spill_table = jax.vmap(place_rows)(partials[:, 1], slot_rows[:, 1])
    coef_table = home_table + jnp.roll(spill_table, -1, axis=0)
    scaled = energies[:, :, :, None] * coef_table
    previous = jnp.roll(scaled, 1, axis=0)

    def select_rows(source, rows):
        return source[rows]

    weights = jnp.stack([jax.vmap(select_rows)(scaled, slot_rows[:, 0]), jax.vmap(select_rows)(previous, slot_rows[:, 1])], axis=1)

    def deposit(footprint, values, coefficient):
        placed = jnp.einsum("sajq,sajo->osaq", values, coefficient, precision=lax.Precision.HIGHEST)
        return jnp.zeros((orbital_count, cell_count), jnp.float32).at[:, footprint].add(placed)

    deposited = jax.vmap(deposit)(support, projectors, weights)
    return deposited.transpose(1, 0, 2).reshape(functions.shape)


def hamiltonian(functions, potential, support, projectors, slot_rows, energies):
    return kinetic(functions) + potential[None] * functions + nonlocal_term(functions, support, projectors, slot_rows, energies)


def reference(orbitals, potential, support, projectors, slot_rows, energies, panel_orbitals):
    applied = hamiltonian(orbitals, potential, support, projectors, slot_rows, energies)
    degree_one = (applied - center_shift * orbitals) / half_width
    applied_two = hamiltonian(degree_one, potential, support, projectors, slot_rows, energies)
    filtered = 2.0 * (applied_two - center_shift * degree_one) / half_width - orbitals
    rounded = filtered.astype(jnp.bfloat16).reshape(filtered.shape[0], -1)
    flat_panel = panel_orbitals.reshape(panel_orbitals.shape[0], -1)
    scale = float(N_DOM * CX * CY * CZ) ** -0.5
    correlation = lax.dot_general(rounded, flat_panel, (((1,), (1,)), ((), ())), preferred_element_type=jnp.float32) * scale
    return filtered, correlation
```

```python
import functools
import math

import jax
import jax.numpy as jnp
from jax import lax
from jax.experimental import pallas as pl
from jax.experimental.pallas import tpu as pltpu
from jax.sharding import PartitionSpec as P

center_shift = 7.5
half_width = 6.5

MESH = pl.DeviceIdType.MESH
I32, F32, BF16 = jnp.int32, jnp.float32, jnp.bfloat16
HIGHEST = lax.Precision.HIGHEST

ORB = 4
ROWS = 192
HALF = 96
PEERS = 16
ATOMS = 48
SUPP = 384
PAIRS = 24
WIDE = 2 * SUPP
CHUNK = ROWS // PEERS
PANEL_DEV = 32
NT = (((1,), (1,)), ((), ()))


def tapered_stencil():
    unscaled = [
        2.0
        * (-1.0) ** (reach + 1)
        * math.sin(math.pi * reach / 8.0)
        / (math.pi * reach / 8.0 * reach * reach)
        for reach in range(1, 7)
    ]
    moment = sum((reach * reach * unscaled[reach - 1] for reach in range(1, 7)))
    side_terms = [neighbour_term / moment for neighbour_term in unscaled]
    return tuple([-2.0 * sum(side_terms)] + side_terms)


def halo_plane(halo, o, x):
    rows = pl.ds(pl.multiple_of(o * HALF, 32) + (x % 3) * 32, 32)
    return halo[rows, (x // 3) * 128 : (x // 3) * 128 + 128].astype(F32)


def local_part(source, low, high, potential, target):
    stencil = tapered_stencil()

    def one(o, carry):
        planes = [halo_plane(low, o, x) for x in range(6)]
        planes += [source[o, x] for x in range(6)]
        planes += [halo_plane(high, o, x) for x in range(6)]
        for x in range(6):
            f = planes[6 + x]
            total = (potential[x] + (-1.5 * stencil[0] - center_shift)) * f
            for k in range(1, 7):
                around = planes[6 + x + k] + planes[6 + x - k]
                around += pltpu.roll(f, k, 0) + pltpu.roll(f, 32 - k, 0)
                around += pltpu.roll(f, k, 1) + pltpu.roll(f, 128 - k, 1)
                total += (-0.5 * stencil[k]) * around
            target[o, x] = total
        return carry

    lax.fori_loop(0, ORB, one, 0)


def to_flat(source, flat):
    for o in range(ORB):
        f = source[o].reshape(ROWS, 128).astype(BF16)
        flat[o * HALF : (o + 1) * HALF, 0:128] = f[:HALF]
        flat[o * HALF : (o + 1) * HALF, 128:256] = f[HALF:]


def build_one(s, u, support, projectors, onehot, line, values):
    t = s * PAIRS + u
    c = jnp.concatenate(
        [support[0, s, pl.ds(2 * u, 1), :], support[0, s, pl.ds(2 * u + 1, 1), :]], axis=1
    )
    values[t] = jnp.concatenate([projectors[0, s, 2 * u], projectors[0, s, 2 * u + 1]], axis=1)
    row = lax.shift_right_logical(c, 7)
    upper = (row >= HALF).astype(I32)
    line[t] = row - HALF * upper
    spot = (c & 127) + 128 * upper
    hit = lax.broadcasted_iota(I32, (256, WIDE), 0) == spot
    onehot[t] = jnp.where(hit, 1.0, 0.0).astype(BF16)


def project(s, flat, onehot, line, values, table):
    lane = lax.broadcasted_iota(I32, (8, 128), 1)

    def body(u, columns):
        t = s * PAIRS + u
        g = jnp.dot(flat[...], onehot[t], preferred_element_type=F32)
        mask = lax.broadcasted_iota(I32, (HALF, WIDE), 0) == line[t]
        p = values[t]
        out = []
        for o in range(ORB):
            picked = jnp.where(mask, g[o * HALF : (o + 1) * HALF], 0.0)
            q = p * jnp.sum(picked, axis=0, keepdims=True)
            first = jnp.sum(q[:, :SUPP], axis=1, keepdims=True)
            second = jnp.sum(q[:, SUPP:], axis=1, keepdims=True)
            column = jnp.where(lane == 2 * u, first, columns[o])
            out.append(jnp.where(lane == 2 * u + 1, second, column))
        return tuple(out)

    start = tuple(jnp.zeros((8, 128), F32) for _ in range(ORB))
    columns = lax.fori_loop(0, PAIRS, body, start, unroll=8)
    return jnp.concatenate(columns, axis=0)


def place(s, weights, onehot, line, values, total):
    lane = lax.broadcasted_iota(I32, (8, 128), 1)

    def body(u, carry):
        t = s * PAIRS + u
        mask = lax.broadcasted_iota(I32, (HALF, WIDE), 0) == line[t]
        p = values[t]
        parts = []
        for o in range(ORB):
            w = weights[s, o * 8 : (o + 1) * 8, :]
            first = jnp.sum(jnp.where(lane == 2 * u, w, 0.0), axis=1, keepdims=True)
            second = jnp.sum(jnp.where(lane == 2 * u + 1, w, 0.0), axis=1, keepdims=True)
            spread = jnp.concatenate(
                [
                    jnp.sum(p[:, :SUPP] * first, axis=0, keepdims=True),
                    jnp.sum(p[:, SUPP:] * second, axis=0, keepdims=True),
                ],
                axis=1,
            )
            parts.append(jnp.where(mask, spread, 0.0).astype(BF16))
        total[...] += lax.dot_general(
            jnp.concatenate(parts, axis=0), onehot[t], NT, preferred_element_type=F32
        )
        return carry

    lax.fori_loop(0, PAIRS, body, 0, unroll=8)


def placed_planes(total, o, x):
    rows = pl.ds(o * HALF + (x % 3) * 32, 32)
    return total[rows, (x // 3) * 128 : (x // 3) * 128 + 128]


def kernel(
    orbitals, potential, support, projectors, slot_rows, energies, panel,
    filtered, correlation,
    onehot, line, values, flat, halo_low, halo_high, table, got, weights, perm, own_slots,
    energy, local, degree_one, total, result, panel_here, ship, landed, spread_rows, gram,
    gram_out, gram_in, red, red_out, red_in,
    halo_send, halo_recv, coef_send, coef_recv, panel_send, panel_recv, keep_sem,
    ship_send, ship_recv, gram_send, gram_recv, red_send, red_recv, out_sem,
):
    band = lax.axis_index("band")
    dom = lax.axis_index("dom")
    right, left = lax.rem(dom + 1, PEERS), lax.rem(dom + PEERS - 1, PEERS)
    barrier = pltpu.get_barrier_semaphore()

    def greet(i, carry):
        pl.semaphore_signal(
            barrier, inc=1, device_id=(lax.rem(band + i, PEERS), dom), device_id_type=MESH
        )
        pl.semaphore_signal(
            barrier, inc=1, device_id=(band, lax.rem(dom + i, PEERS)), device_id_type=MESH
        )
        return carry

    lax.fori_loop(1, PEERS, greet, 0)

    to_flat(orbitals, flat.at[0])

    def build(u, carry):
        build_one(0, u, support, projectors, onehot, line, values)
        build_one(1, u, support, projectors, onehot, line, values)
        return carry

    lax.fori_loop(0, PAIRS, build, 0)
    own_slots[...] = jnp.full((2, 8, 128), -1, I32)
    energy[...] = jnp.zeros((2, 8, 128), F32)
    eye = (
        lax.broadcasted_iota(I32, (8, 8), 0) == lax.broadcasted_iota(I32, (8, 8), 1)
    ).astype(F32)
    for s, block in ((0, dom), (1, left)):
        own_slots[s, 0:1, 0:ATOMS] = slot_rows[0, s : s + 1, :]
        hit = lax.broadcasted_iota(I32, (128, 128), 0) == own_slots[s, 0:1, :]
        perm[s] = jnp.where(hit, 1.0, 0.0)
        energy[s, :, 0:ATOMS] = lax.dot_general(
            eye, energies[block], NT, precision=HIGHEST, preferred_element_type=F32
        )

    pl.semaphore_wait(barrier, 2 * (PEERS - 1))

    def to_side(source, target, send, recv, side):
        return pltpu.make_async_remote_copy(
            src_ref=source, dst_ref=target, send_sem=send, recv_sem=recv,
            device_id=(band, side), device_id_type=MESH,
        )

    def halo_copies(d):
        return (
            to_side(flat.at[d], halo_low.at[d], halo_send.at[d, 0], halo_recv.at[d, 0], right),
            to_side(flat.at[d], halo_high.at[d], halo_send.at[d, 1], halo_recv.at[d, 1], left),
        )

    def coef_copy(d, s):
        return to_side(
            table.at[d, s], got.at[d, s], coef_send.at[d, s], coef_recv.at[d, s],
            left if s else right,
        )

    def panel_copy(i):
        peer = lax.rem(band + i, PEERS)
        return pltpu.make_async_remote_copy(
            src_ref=panel.at[pl.ds(peer * CHUNK, CHUNK)],
            dst_ref=panel_here.at[:, pl.ds(pl.multiple_of(band * PANEL_DEV, PANEL_DEV), PANEL_DEV), :],
            send_sem=panel_send.at[i], recv_sem=panel_recv.at[i],
            device_id=(peer, dom), device_id_type=MESH,
        )

    keep = pltpu.make_async_copy(
        panel.at[pl.ds(band * CHUNK, CHUNK)],
        panel_here.at[:, pl.ds(pl.multiple_of(band * PANEL_DEV, PANEL_DEV), PANEL_DEV), :],
        keep_sem,
    )

    def each(copy_of, action):
        def body(i, carry):
            getattr(copy_of(i), action)()
            return carry

        lax.fori_loop(1, PEERS, body, 0)

    for copy in halo_copies(0):
        copy.start()
    keep.start()
    each(panel_copy, "start")

    def apply(d, source):
        for s in (1, 0):
            columns = project(s, flat.at[d], onehot, line, values, table)
            table[d, s] = lax.dot_general(
                columns, perm[s], NT, precision=HIGHEST, preferred_element_type=F32
            )
            coef_copy(d, s).start()
        for copy in halo_copies(d):
            copy.wait_recv()
        local_part(source, halo_low.at[d], halo_high.at[d], potential, local)
        total[...] = jnp.zeros(total.shape, F32)
        for s in (0, 1):
            coef_copy(d, 1 - s).wait_recv()
            scaled = jnp.concatenate([energy[s]] * ORB, axis=0) * (table[d, s] + got[d, 1 - s])
            weights[s] = jnp.dot(scaled, perm[s], precision=HIGHEST, preferred_element_type=F32)
            place(s, weights, onehot, line, values, total)

    apply(0, orbitals)
    for o in range(ORB):
        for x in range(6):
            degree_one[o, x] = (local[o, x] + placed_planes(total, o, x)) * (1.0 / half_width)
    to_flat(degree_one, flat.at[1])
    for copy in halo_copies(1):
        copy.start()

    apply(1, degree_one)
    for o in range(ORB):
        for x in range(6):
            new = (local[o, x] + placed_planes(total, o, x)) * (2.0 / half_width) - orbitals[o, x]
            degree_one[o, x] = new
            result[o, x * 32 : (x + 1) * 32, :] = new
    write = pltpu.make_async_copy(degree_one, filtered, out_sem)
    write.start()

    for c in range(PEERS):
        for o in range(ORB):
            spread_rows[c * ORB * CHUNK + o * CHUNK : c * ORB * CHUNK + (o + 1) * CHUNK, :] = result[
                o, c * CHUNK : (c + 1) * CHUNK, :
            ]
        ship[c] = spread_rows[c * ORB * CHUNK : (c + 1) * ORB * CHUNK, :].astype(BF16)

    def ship_copy(i):
        peer = lax.rem(band + i, PEERS)
        return pltpu.make_async_remote_copy(
            src_ref=ship.at[peer], dst_ref=landed.at[band],
            send_sem=ship_send.at[i], recv_sem=ship_recv.at[i],
            device_id=(peer, dom), device_id_type=MESH,
        )

    each(ship_copy, "start")
    landed[band] = ship[band]
    keep.wait()
    each(panel_copy, "wait_recv")
    each(ship_copy, "wait_recv")

    for c in range(PEERS):
        spread_rows[c * ORB * CHUNK : (c + 1) * ORB * CHUNK, :] = landed[c].astype(F32)
    products = jnp.zeros((ORB * PEERS, PEERS * PANEL_DEV), F32)
    for k in range(0, CHUNK, 2):
        lines = [
            jnp.concatenate(
                [
                    spread_rows[pl.ds(o * CHUNK + n, PEERS, stride=ORB * CHUNK), :]
                    for o in range(ORB)
                ],
                axis=0,
            )
            for n in (k, k + 1)
        ]
        products += lax.dot_general(
            jnp.concatenate(lines, axis=1).astype(BF16),
            jnp.concatenate([panel_here[k], panel_here[k + 1]], axis=1),
            NT,
            preferred_element_type=F32,
        )
    for n in range(4):
        gram[n] = products[:, n * 128 : (n + 1) * 128]

    for d in range(PEERS):
        for n in range(4):
            gram_out[
                d, (n // 2) * ORB : (n // 2) * ORB + ORB, (n % 2) * 128 : (n % 2) * 128 + 128
            ] = gram[n, pl.ds(d, ORB, stride=PEERS), :]

    def gram_copy(i):
        peer = lax.rem(dom + i, PEERS)
        return pltpu.make_async_remote_copy(
            src_ref=gram_out.at[peer], dst_ref=gram_in.at[dom],
            send_sem=gram_send.at[i], recv_sem=gram_recv.at[i],
            device_id=(band, peer), device_id_type=MESH,
        )

    each(gram_copy, "start")
    gram_in[dom] = gram_out[dom]
    each(gram_copy, "wait_recv")
    red[...] = jnp.sum(gram_in[...], axis=0)
    red_out[...] = jnp.zeros(red_out.shape, F32)
    for b in range(PEERS):
        half, at = b // 8, (b % 8) * PANEL_DEV
        red_out[b, 0:ORB, 0:PANEL_DEV] = red[half * ORB : (half + 1) * ORB, at : at + PANEL_DEV]

    def red_copy(i):
        peer = lax.rem(band + i, PEERS)
        return pltpu.make_async_remote_copy(
            src_ref=red_out.at[peer], dst_ref=red_in.at[band],
            send_sem=red_send.at[i], recv_sem=red_recv.at[i],
            device_id=(peer, dom), device_id_type=MESH,
        )

    each(red_copy, "start")
    red_in[band] = red_out[band]
    each(red_copy, "wait_recv")
    scale = float(PEERS * ROWS * 128) ** (-0.5)
    correlation[...] = jnp.sum(red_in[...], axis=0)[0:ORB, 0:PANEL_DEV] * scale

    write.wait()
    for d in range(2):
        for copy in halo_copies(d):
            copy.wait_send()
        for s in range(2):
            coef_copy(d, s).wait_send()
    for copy_of in (panel_copy, ship_copy, gram_copy, red_copy):
        each(copy_of, "wait_send")


def per_device(orbitals, potential, support, projectors, slot_rows, energies, panel_orbitals):
    lines = panel_orbitals.reshape(PANEL_DEV, ROWS, 128).transpose(1, 0, 2)
    vmem = pl.BlockSpec(memory_space=pltpu.VMEM)
    anywhere = pl.BlockSpec(memory_space=pl.ANY)
    dma = pltpu.SemaphoreType.DMA
    return pl.pallas_call(
        kernel,
        out_shape=(
            jax.ShapeDtypeStruct((ORB, 6, 32, 128), F32),
            jax.ShapeDtypeStruct((ORB, PANEL_DEV), F32),
        ),
        in_specs=[vmem] * 6 + [anywhere],
        out_specs=(anywhere, vmem),
        scratch_shapes=[
            pltpu.VMEM((2 * PAIRS, 256, WIDE), BF16),
            pltpu.VMEM((2 * PAIRS, 1, WIDE), I32),
            pltpu.VMEM((2 * PAIRS, 8, WIDE), F32),
            pltpu.VMEM((2, ORB * HALF, 256), BF16),
            pltpu.VMEM((2, ORB * HALF, 256), BF16),
            pltpu.VMEM((2, ORB * HALF, 256), BF16),
            pltpu.VMEM((2, 2, ORB * 8, 128), F32),
            pltpu.VMEM((2, 2, ORB * 8, 128), F32),
            pltpu.VMEM((2, ORB * 8, 128), F32),
            pltpu.VMEM((2, 128, 128), F32),
            pltpu.VMEM((2, 8, 128), I32),
            pltpu.VMEM((2, 8, 128), F32),
            pltpu.VMEM((ORB, 6, 32, 128), F32),
            pltpu.VMEM((ORB, 6, 32, 128), F32),
            pltpu.VMEM((ORB * HALF, 256), F32),
            pltpu.VMEM((ORB, ROWS, 128), F32),
            pltpu.VMEM((CHUNK, PEERS * PANEL_DEV, 128), BF16),
            pltpu.VMEM((PEERS, ORB * CHUNK, 128), BF16),
            pltpu.VMEM((PEERS, ORB * CHUNK, 128), BF16),
            pltpu.VMEM((PEERS * ORB * CHUNK, 128), F32),
            pltpu.VMEM((4, ORB * PEERS, 128), F32),
            pltpu.VMEM((PEERS, 2 * ORB, 256), F32),
            pltpu.VMEM((PEERS, 2 * ORB, 256), F32),
            pltpu.VMEM((2 * ORB, 256), F32),
            pltpu.VMEM((PEERS, 8, 128), F32),
            pltpu.VMEM((PEERS, 8, 128), F32),
            dma((2, 2)), dma((2, 2)),
            dma((2, 2)), dma((2, 2)),
            dma((PEERS,)), dma((PEERS,)), dma,
            dma((PEERS,)), dma((PEERS,)),
            dma((PEERS,)), dma((PEERS,)),
            dma((PEERS,)), dma((PEERS,)),
            dma,
        ],
        compiler_params=pltpu.CompilerParams(
            collective_id=0, has_side_effects=True, vmem_limit_bytes=60 * 2**20
        ),
    )(orbitals, potential, support, projectors, slot_rows, energies, lines)


def solution(mesh):
    return jax.shard_map(
        per_device,
        mesh=mesh,
        in_specs=(
            P("band", "dom", None, None),
            P("dom", None, None),
            P("dom", None, None, None),
            P("dom", None, None, None, None),
            P("dom", None, None),
            P(),
            P("band", "dom", None, None),
        ),
        out_specs=(P("band", "dom", None, None), P("dom", "band")),
        check_vma=False,
    )
```

```python
import math

import jax
import jax.numpy as jnp
from jax import lax
from jax.experimental import pallas as pl
from jax.experimental.pallas import tpu as pltpu
from jax.sharding import PartitionSpec as P

center_shift = 7.5
half_width = 6.5

MESH = pl.DeviceIdType.MESH
I32, F32, BF16, F8 = jnp.int32, jnp.float32, jnp.bfloat16, jnp.float8_e4m3fn
HIGHEST = lax.Precision.HIGHEST

ORB = 4
ROWS = 192
STRIP = 48
TOP = 224.0
UNROLL = 8
PEERS = 16
ATOMS = 48
SUPP = 384
PAIRS = 24
WIDE = 2 * SUPP
CHUNK = ROWS // PEERS
PANEL_DEV = 32
NT = (((1,), (1,)), ((), ()))


def tapered_stencil():
    unscaled = [
        2.0
        * (-1.0) ** (reach + 1)
        * math.sin(math.pi * reach / 8.0)
        / (math.pi * reach / 8.0 * reach * reach)
        for reach in range(1, 7)
    ]
    moment = sum((reach * reach * unscaled[reach - 1] for reach in range(1, 7)))
    side_terms = [neighbour_term / moment for neighbour_term in unscaled]
    return tuple([-2.0 * sum(side_terms)] + side_terms)


def local_part(source, low, high, potential, target):
    stencil = tapered_stencil()

    def one(o, carry):
        planes = [low[o, x].astype(F32) for x in range(6)]
        planes += [source[o, x] for x in range(6)]
        planes += [high[o, x].astype(F32) for x in range(6)]
        for x in range(6):
            f = planes[6 + x]
            total = (potential[x] + (-1.5 * stencil[0] - center_shift)) * f
            for k in range(1, 7):
                around = planes[6 + x + k] + planes[6 + x - k]
                around += pltpu.roll(f, k, 0) + pltpu.roll(f, 32 - k, 0)
                around += pltpu.roll(f, k, 1) + pltpu.roll(f, 128 - k, 1)
                total += (-0.5 * stencil[k]) * around
            target[o, x] = total
        return carry

    lax.fori_loop(0, ORB, one, 0)


def two_terms(x):
    first = x.astype(F8).astype(F32)
    return first, x - first


def peak(x):
    return jnp.max(jnp.max(jnp.abs(x), axis=0, keepdims=True), axis=1, keepdims=True)


def to_flat(source, flat, sent):
    back, terms = [], []
    for o in range(ORB):
        f = source[o]
        sent[o] = f.astype(BF16)
        top = jnp.maximum(peak(f.reshape(ROWS, 128)), 1e-30)
        back.append(top * (1.0 / TOP))
        terms.append(two_terms(f * (TOP / top)[None]))
    for n in range(2):
        for q in range(4):
            strip = [t[n][:, 8 * q : 8 * q + 8, :].reshape(STRIP, 128) for t in terms]
            flat[n * ORB * STRIP : (n + 1) * ORB * STRIP, q * 128 : (q + 1) * 128] = (
                jnp.concatenate(strip, axis=0).astype(F8)
            )
    return back


def onehot_of(spot):
    wide = jnp.broadcast_to(spot, (16, WIDE))
    upper = wide >= 256
    low = jnp.where(upper, -1.0, wide.astype(F32)).astype(BF16)
    high = jnp.where(upper, (wide - 256).astype(F32), -1.0).astype(BF16)
    count = lax.broadcasted_iota(I32, (16, WIDE), 0).astype(F32).astype(BF16)
    one, zero = jnp.array(1, BF16), jnp.array(0, BF16)
    parts = [
        jnp.where(count + jnp.array(16.0 * k, BF16) == side, one, zero)
        for side in (low, high)
        for k in range(16)
    ]
    return jnp.concatenate(parts, axis=0).astype(F8)


def build_one(s, u, support, projectors, onehot, line, values):
    t = s * PAIRS + u
    c = jnp.concatenate(
        [support[0, s, pl.ds(2 * u, 1), :], support[0, s, pl.ds(2 * u + 1, 1), :]], axis=1
    )
    values[t] = jnp.concatenate([projectors[0, s, 2 * u], projectors[0, s, 2 * u + 1]], axis=1)
    line[t] = lax.shift_right_logical(c, 12) * 8 + (lax.shift_right_logical(c, 7) & 7)
    hot = onehot_of((c & 127) + (lax.shift_right_logical(c, 10) & 3) * 128)
    onehot[t] = hot
    return hot


def project(s, flat, onehot, line, values, build, extra):
    lane = lax.broadcasted_iota(I32, (8, 128), 1)

    def body(u, state):
        columns, largest = state
        t = s * PAIRS + u
        if build is None:
            hot = onehot[t]
        else:
            hot = build(s, u)
        extra(s, u)
        g = jnp.dot(flat[...], hot, preferred_element_type=F32)
        mask = lax.broadcasted_iota(I32, (STRIP, WIDE), 0) == line[t]
        p = values[t]
        if build is not None:
            for n in range(6):
                largest = jnp.maximum(largest, jnp.abs(p[:, n * 128 : (n + 1) * 128]))
        out = []
        for o in range(ORB):
            both = (
                g[o * STRIP : (o + 1) * STRIP]
                + g[(ORB + o) * STRIP : (ORB + o + 1) * STRIP]
            )
            q = p * jnp.sum(jnp.where(mask, both, 0.0), axis=0, keepdims=True)
            first = jnp.sum(q[:, :SUPP], axis=1, keepdims=True)
            second = jnp.sum(q[:, SUPP:], axis=1, keepdims=True)
            column = jnp.where(lane == 2 * u, first, columns[o])
            out.append(jnp.where(lane == 2 * u + 1, second, column))
        return tuple(out), largest

    start = tuple(jnp.zeros((8, 128), F32) for _ in range(ORB)), jnp.zeros((8, 128), F32)
    return lax.fori_loop(0, PAIRS, body, start, unroll=UNROLL)


def place(s, weights, onehot, line, values, total):
    lane = lax.broadcasted_iota(I32, (8, 128), 1)

    def body(u, carry):
        t = s * PAIRS + u
        mask = lax.broadcasted_iota(I32, (STRIP, WIDE), 0) == line[t]
        p = values[t]
        firsts, seconds = [], []
        for o in range(ORB):
            w = weights[s, o * 8 : (o + 1) * 8, :]
            left = jnp.sum(jnp.where(lane == 2 * u, w, 0.0), axis=1, keepdims=True)
            right = jnp.sum(jnp.where(lane == 2 * u + 1, w, 0.0), axis=1, keepdims=True)
            spread = jnp.concatenate(
                [
                    jnp.sum(p[:, :SUPP] * left, axis=0, keepdims=True),
                    jnp.sum(p[:, SUPP:] * right, axis=0, keepdims=True),
                ],
                axis=1,
            )
            first, second = two_terms(spread)
            firsts.append(jnp.where(mask, first, 0.0))
            seconds.append(jnp.where(mask, second, 0.0))
        g = lax.dot_general(
            jnp.concatenate(firsts + seconds, axis=0).astype(F8),
            onehot[t],
            NT,
            preferred_element_type=F32,
        )
        total[s] += g[: ORB * STRIP] + g[ORB * STRIP :]
        return carry

    lax.fori_loop(0, PAIRS, body, 0, unroll=UNROLL)


def placed_planes(total, back, o, x):
    rows = slice(o * STRIP + 8 * x, o * STRIP + 8 * x + 8)
    return jnp.concatenate(
        [
            total[0, rows, q * 128 : (q + 1) * 128] * back[0][o]
            + total[1, rows, q * 128 : (q + 1) * 128] * back[1][o]
            for q in range(4)
        ],
        axis=0,
    )


def kernel(
    orbitals, potential, support, projectors, slot_rows, energies, panel,
    filtered, sums,
    onehot, line, values, flat, sent, halo_low, halo_high, table, got, weights, perm, own_slots,
    energy, local, degree_one, total, result, panel_raw, panel_wide, panel_lines, panel_here,
    ship, landed, spread_rows, gram,
    gram_out, gram_in, red, red_out, red_in,
    halo_send, halo_recv, coef_send, coef_recv, panel_send, panel_recv, keep_sem, panel_sem,
    ship_send, ship_recv, gram_send, gram_recv, red_send, red_recv, out_sem,
):
    band = lax.axis_index("band")
    dom = lax.axis_index("dom")
    right, left = lax.rem(dom + 1, PEERS), lax.rem(dom + PEERS - 1, PEERS)
    barrier = pltpu.get_barrier_semaphore()

    def greet(i, carry):
        pl.semaphore_signal(
            barrier, inc=1, device_id=(lax.rem(band + i, PEERS), dom), device_id_type=MESH
        )
        pl.semaphore_signal(
            barrier, inc=1, device_id=(band, lax.rem(dom + i, PEERS)), device_id_type=MESH
        )
        return carry

    lax.fori_loop(1, PEERS, greet, 0)

    fetch = pltpu.make_async_copy(panel, panel_raw, panel_sem)
    fetch.start()
    back_one = to_flat(orbitals, flat, sent.at[0])
    own_slots[...] = jnp.full((2, 8, 128), -1, I32)
    energy[...] = jnp.zeros((2, 8, 128), F32)
    for s, block in ((0, dom), (1, left)):
        own_slots[s, 0:1, 0:ATOMS] = slot_rows[0, s : s + 1, :]
        hit = lax.broadcasted_iota(I32, (128, 128), 0) == own_slots[s, 0:1, :]
        perm[s] = jnp.where(hit, 1.0, 0.0)
        energy[s, :, 0:ATOMS] = energies[block]
    fetch.wait()

    pl.semaphore_wait(barrier, 2 * (PEERS - 1))

    def to_side(source, target, send, recv, side):
        return pltpu.make_async_remote_copy(
            src_ref=source, dst_ref=target, send_sem=send, recv_sem=recv,
            device_id=(band, side), device_id_type=MESH,
        )

    def halo_copies(d):
        return (
            to_side(sent.at[d], halo_low.at[d], halo_send.at[d, 0], halo_recv.at[d, 0], right),
            to_side(sent.at[d], halo_high.at[d], halo_send.at[d, 1], halo_recv.at[d, 1], left),
        )

    def coef_copy(d, s):
        return to_side(
            table.at[d, s], got.at[d, s], coef_send.at[d, s], coef_recv.at[d, s],
            left if s else right,
        )

    def panel_copy(i):
        peer = lax.rem(band + i, PEERS)
        return pltpu.make_async_remote_copy(
            src_ref=panel_lines.at[pl.ds(peer * CHUNK, CHUNK)],
            dst_ref=panel_here.at[:, pl.ds(pl.multiple_of(band * PANEL_DEV, PANEL_DEV), PANEL_DEV), :],
            send_sem=panel_send.at[i], recv_sem=panel_recv.at[i],
            device_id=(peer, dom), device_id_type=MESH,
        )

    keep = pltpu.make_async_copy(
        panel_lines.at[pl.ds(band * CHUNK, CHUNK)],
        panel_here.at[:, pl.ds(pl.multiple_of(band * PANEL_DEV, PANEL_DEV), PANEL_DEV), :],
        keep_sem,
    )

    def each(copy_of, action):
        def body(i, carry):
            getattr(copy_of(i), action)()
            return carry

        lax.fori_loop(1, PEERS, body, 0)

    for copy in halo_copies(0):
        copy.start()

    def build(s, u):
        return build_one(s, u, support, projectors, onehot, line, values)

    def turn_panel(s, u):
        if s == 1:
            for n in range(8):
                plane = u * 8 + n
                panel_wide[pl.ds(pl.multiple_of(plane * 32, 32), 32), :] = panel_raw[
                    plane // 6, plane % 6
                ].astype(F32)
        else:
            for n in range(8):
                row = u * 8 + n
                panel_lines[row] = panel_wide[
                    pl.ds(row, PANEL_DEV, stride=ROWS), :
                ].astype(BF16)

    def nothing(s, u):
        pass

    def apply(d, source, back, build, extra, after, largest):
        found = []
        for s in (1, 0):
            columns, peaks = project(s, flat, onehot, line, values, build, extra)
            found.append(peaks)
            columns = jnp.concatenate([columns[o] * back[o] for o in range(ORB)], axis=0)
            table[d, s] = lax.dot_general(
                columns, perm[s], NT, precision=HIGHEST, preferred_element_type=F32
            )
            coef_copy(d, s).start()
        after()
        if largest is None:
            largest = jnp.max(jnp.maximum(found[0], found[1]), axis=1, keepdims=True)
        for copy in halo_copies(d):
            copy.wait_recv()
        local_part(source, halo_low.at[d], halo_high.at[d], potential, local)
        total[...] = jnp.zeros(total.shape, F32)
        scales = []
        for s in (0, 1):
            coef_copy(d, 1 - s).wait_recv()
            scaled = jnp.concatenate([energy[s]] * ORB, axis=0) * (table[d, s] + got[d, 1 - s])
            own = jnp.dot(scaled, perm[s], precision=HIGHEST, preferred_element_type=F32)
            scales.append([])
            for o in range(ORB):
                w = own[o * 8 : (o + 1) * 8, :]
                most = jnp.sum(jnp.abs(w) * largest, axis=0, keepdims=True)
                most = jnp.maximum(jnp.max(most, axis=1, keepdims=True), 1e-30)
                weights[s, o * 8 : (o + 1) * 8, :] = w * (TOP / most)
                scales[s].append(most * (1.0 / TOP))
            place(s, weights, onehot, line, values, total)
        return largest, scales

    def send_panel():
        keep.start()
        each(panel_copy, "start")

    largest, scales = apply(0, orbitals, back_one, build, turn_panel, send_panel, None)
    for o in range(ORB):
        for x in range(6):
            degree_one[o, x] = (local[o, x] + placed_planes(total, scales, o, x)) * (
                1.0 / half_width
            )
    back_two = to_flat(degree_one, flat, sent.at[1])
    for copy in halo_copies(1):
        copy.start()

    largest, scales = apply(1, degree_one, back_two, None, nothing, lambda: None, largest)
    for o in range(ORB):
        for x in range(6):
            new = (local[o, x] + placed_planes(total, scales, o, x)) * (
                2.0 / half_width
            ) - orbitals[o, x]
            degree_one[o, x] = new
            result[o, x * 32 : (x + 1) * 32, :] = new
    write = pltpu.make_async_copy(degree_one, filtered, out_sem)
    write.start()

    for c in range(PEERS):
        for o in range(ORB):
            spread_rows[c * ORB * CHUNK + o * CHUNK : c * ORB * CHUNK + (o + 1) * CHUNK, :] = result[
                o, c * CHUNK : (c + 1) * CHUNK, :
            ]
        ship[c] = spread_rows[c * ORB * CHUNK : (c + 1) * ORB * CHUNK, :].astype(BF16)

    def ship_copy(i):
        peer = lax.rem(band + i, PEERS)
        return pltpu.make_async_remote_copy(
            src_ref=ship.at[peer], dst_ref=landed.at[band],
            send_sem=ship_send.at[i], recv_sem=ship_recv.at[i],
            device_id=(peer, dom), device_id_type=MESH,
        )

    each(ship_copy, "start")
    landed[band] = ship[band]
    keep.wait()
    each(panel_copy, "wait_recv")
    each(ship_copy, "wait_recv")

    for c in range(PEERS):
        spread_rows[c * ORB * CHUNK : (c + 1) * ORB * CHUNK, :] = landed[c].astype(F32)
    products = jnp.zeros((ORB * PEERS, PEERS * PANEL_DEV), F32)
    for k in range(0, CHUNK, 2):
        lines = [
            jnp.concatenate(
                [
                    spread_rows[pl.ds(o * CHUNK + n, PEERS, stride=ORB * CHUNK), :]
                    for o in range(ORB)
                ],
                axis=0,
            )
            for n in (k, k + 1)
        ]
        products += lax.dot_general(
            jnp.concatenate(lines, axis=1).astype(BF16),
            jnp.concatenate([panel_here[k], panel_here[k + 1]], axis=1),
            NT,
            preferred_element_type=F32,
        )
    for n in range(4):
        gram[n] = products[:, n * 128 : (n + 1) * 128]

    for d in range(PEERS):
        for n in range(4):
            gram_out[
                d, (n // 2) * ORB : (n // 2) * ORB + ORB, (n % 2) * 128 : (n % 2) * 128 + 128
            ] = gram[n, pl.ds(d, ORB, stride=PEERS), :]

    def gram_copy(i):
        peer = lax.rem(dom + i, PEERS)
        return pltpu.make_async_remote_copy(
            src_ref=gram_out.at[peer], dst_ref=gram_in.at[dom],
            send_sem=gram_send.at[i], recv_sem=gram_recv.at[i],
            device_id=(band, peer), device_id_type=MESH,
        )

    each(gram_copy, "start")
    gram_in[dom] = gram_out[dom]
    each(gram_copy, "wait_recv")
    red[...] = jnp.sum(gram_in[...], axis=0)
    red_out[...] = jnp.zeros(red_out.shape, F32)
    for b in range(PEERS):
        half, at = b // 8, (b % 8) * PANEL_DEV
        red_out[b, 0:ORB, 0:PANEL_DEV] = red[half * ORB : (half + 1) * ORB, at : at + PANEL_DEV]

    def red_copy(i):
        peer = lax.rem(band + i, PEERS)
        return pltpu.make_async_remote_copy(
            src_ref=red_out.at[peer], dst_ref=red_in.at[band],
            send_sem=red_send.at[i], recv_sem=red_recv.at[i],
            device_id=(peer, dom), device_id_type=MESH,
        )

    each(red_copy, "start")
    red_in[band] = red_out[band]
    each(red_copy, "wait_recv")
    sums[...] = jnp.sum(red_in[...], axis=0)

    write.wait()
    for d in range(2):
        for copy in halo_copies(d):
            copy.wait_send()
        for s in range(2):
            coef_copy(d, s).wait_send()
    for copy_of in (panel_copy, ship_copy, gram_copy, red_copy):
        each(copy_of, "wait_send")


def finish(raw, sums, filtered, correlation):
    filtered[...] = raw[...]
    correlation[...] = sums[0:ORB, 0:PANEL_DEV] * float(PEERS * ROWS * 128) ** (-0.5)


def per_device(orbitals, potential, support, projectors, slot_rows, energies, panel_orbitals):
    vmem = pl.BlockSpec(memory_space=pltpu.VMEM)
    anywhere = pl.BlockSpec(memory_space=pl.ANY)
    dma = pltpu.SemaphoreType.DMA
    raw, sums = pl.pallas_call(
        kernel,
        out_shape=(
            jax.ShapeDtypeStruct((ORB, 6, 32, 128), F32),
            jax.ShapeDtypeStruct((8, 128), F32),
        ),
        in_specs=[vmem] * 6 + [anywhere],
        out_specs=(anywhere, vmem),
        scratch_shapes=[
            pltpu.VMEM((2 * PAIRS, 512, WIDE), F8),
            pltpu.VMEM((2 * PAIRS, 1, WIDE), I32),
            pltpu.VMEM((2 * PAIRS, 8, WIDE), F32),
            pltpu.VMEM((2 * ORB * STRIP, 512), F8),
            pltpu.VMEM((2, ORB, 6, 32, 128), BF16),
            pltpu.VMEM((2, ORB, 6, 32, 128), BF16),
            pltpu.VMEM((2, ORB, 6, 32, 128), BF16),
            pltpu.VMEM((2, 2, ORB * 8, 128), F32),
            pltpu.VMEM((2, 2, ORB * 8, 128), F32),
            pltpu.VMEM((2, ORB * 8, 128), F32),
            pltpu.VMEM((2, 128, 128), F32),
            pltpu.VMEM((2, 8, 128), I32),
            pltpu.VMEM((2, 8, 128), F32),
            pltpu.VMEM((ORB, 6, 32, 128), F32),
            pltpu.VMEM((ORB, 6, 32, 128), F32),
            pltpu.VMEM((2, ORB * STRIP, 512), F32),
            pltpu.VMEM((ORB, ROWS, 128), F32),
            pltpu.VMEM((PANEL_DEV, 6, 32, 128), BF16),
            pltpu.VMEM((PANEL_DEV * ROWS, 128), F32),
            pltpu.VMEM((ROWS, PANEL_DEV, 128), BF16),
            pltpu.VMEM((CHUNK, PEERS * PANEL_DEV, 128), BF16),
            pltpu.VMEM((PEERS, ORB * CHUNK, 128), BF16),
            pltpu.VMEM((PEERS, ORB * CHUNK, 128), BF16),
            pltpu.VMEM((PEERS * ORB * CHUNK, 128), F32),
            pltpu.VMEM((4, ORB * PEERS, 128), F32),
            pltpu.VMEM((PEERS, 2 * ORB, 256), F32),
            pltpu.VMEM((PEERS, 2 * ORB, 256), F32),
            pltpu.VMEM((2 * ORB, 256), F32),
            pltpu.VMEM((PEERS, 8, 128), F32),
            pltpu.VMEM((PEERS, 8, 128), F32),
            dma((2, 2)), dma((2, 2)),
            dma((2, 2)), dma((2, 2)),
            dma((PEERS,)), dma((PEERS,)), dma, dma,
            dma((PEERS,)), dma((PEERS,)),
            dma((PEERS,)), dma((PEERS,)),
            dma((PEERS,)), dma((PEERS,)),
            dma,
        ],
        compiler_params=pltpu.CompilerParams(
            collective_id=0, has_side_effects=True, vmem_limit_bytes=60 * 2**20
        ),
    )(
        orbitals,
        potential,
        support,
        projectors,
        slot_rows,
        energies.transpose(0, 2, 1),
        panel_orbitals,
    )
    return pl.pallas_call(
        finish,
        out_shape=(
            jax.ShapeDtypeStruct((ORB, 6, 32, 128), F32),
            jax.ShapeDtypeStruct((ORB, PANEL_DEV), F32),
        ),
        in_specs=[vmem] * 2,
        out_specs=(vmem, vmem),
    )(raw, sums)


def solution(mesh):
    return jax.shard_map(
        per_device,
        mesh=mesh,
        in_specs=(
            P("band", "dom", None, None),
            P("dom", None, None),
            P("dom", None, None, None),
            P("dom", None, None, None, None),
            P("dom", None, None),
            P(),
            P("band", "dom", None, None),
        ),
        out_specs=(P("band", "dom", None, None), P("dom", "band")),
        check_vma=False,
    )
```

```python
import math

import jax
import jax.numpy as jnp
from jax import lax
from jax.experimental import pallas as pl
from jax.experimental.pallas import tpu as pltpu
from jax.sharding import PartitionSpec as P

center_shift = 7.5
half_width = 6.5

MESH = pl.DeviceIdType.MESH
I32, F32, BF16, F8 = jnp.int32, jnp.float32, jnp.bfloat16, jnp.float8_e4m3fn
HIGHEST = lax.Precision.HIGHEST

ORB = 4
ROWS = 192
STRIP = 48
TOP = 224.0
GROUP = 12
PEERS = 16
ATOMS = 48
SUPP = 384
PAIRS = 24
WIDE = 2 * SUPP
CHUNK = ROWS // PEERS
PANEL_DEV = 32
NT = (((1,), (1,)), ((), ()))


def tapered_stencil():
    unscaled = [
        2.0
        * (-1.0) ** (reach + 1)
        * math.sin(math.pi * reach / 8.0)
        / (math.pi * reach / 8.0 * reach * reach)
        for reach in range(1, 7)
    ]
    moment = sum((reach * reach * unscaled[reach - 1] for reach in range(1, 7)))
    side_terms = [neighbour_term / moment for neighbour_term in unscaled]
    return tuple([-2.0 * sum(side_terms)] + side_terms)


def local_part(source, low, high, potential, target):
    stencil = tapered_stencil()

    def one(o, carry):
        planes = [low[o, x].astype(F32) for x in range(6)]
        planes += [source[o, x] for x in range(6)]
        planes += [high[o, x].astype(F32) for x in range(6)]
        for x in range(6):
            f = planes[6 + x]
            total = (potential[x] + (-1.5 * stencil[0] - center_shift)) * f
            for k in range(1, 7):
                around = planes[6 + x + k] + planes[6 + x - k]
                around += pltpu.roll(f, k, 0) + pltpu.roll(f, 32 - k, 0)
                around += pltpu.roll(f, k, 1) + pltpu.roll(f, 128 - k, 1)
                total += (-0.5 * stencil[k]) * around
            target[o, x] = total
        return carry

    lax.fori_loop(0, ORB, one, 0)


def two_terms(x):
    first = x.astype(F8).astype(F32)
    return first, x - first


def peak(x):
    return jnp.max(jnp.max(jnp.abs(x), axis=0, keepdims=True), axis=1, keepdims=True)


def to_flat(source, flat, sent):
    back, terms = [], []
    for o in range(ORB):
        f = source[o]
        sent[o] = f.astype(BF16)
        top = jnp.maximum(peak(f.reshape(ROWS, 128)), 1e-30)
        back.append(top * (1.0 / TOP))
        terms.append(two_terms(f * (TOP / top)[None]))
    for n in range(2):
        for q in range(4):
            strip = [t[n][:, 8 * q : 8 * q + 8, :].reshape(STRIP, 128) for t in terms]
            flat[n * ORB * STRIP : (n + 1) * ORB * STRIP, q * 128 : (q + 1) * 128] = (
                jnp.concatenate(strip, axis=0).astype(F8)
            )
    return back


def onehot_of(spot):
    wide = jnp.broadcast_to(spot, (16, WIDE))
    upper = wide >= 256
    low = jnp.where(upper, -1.0, wide.astype(F32)).astype(BF16)
    high = jnp.where(upper, (wide - 256).astype(F32), -1.0).astype(BF16)
    count = lax.broadcasted_iota(I32, (16, WIDE), 0).astype(F32).astype(BF16)
    one, zero = jnp.array(1, BF16), jnp.array(0, BF16)
    parts = [
        jnp.where(count + jnp.array(16.0 * k, BF16) == side, one, zero)
        for side in (low, high)
        for k in range(16)
    ]
    return jnp.concatenate(parts, axis=0).astype(F8)


def build_one(s, u, support, projectors, onehot, line, values):
    t = s * PAIRS + u
    c = jnp.concatenate(
        [support[0, s, pl.ds(2 * u, 1), :], support[0, s, pl.ds(2 * u + 1, 1), :]], axis=1
    )
    values[t] = jnp.concatenate([projectors[0, s, 2 * u], projectors[0, s, 2 * u + 1]], axis=1)
    line[t] = lax.shift_right_logical(c, 12) * 8 + (lax.shift_right_logical(c, 7) & 7)
    hot = onehot_of((c & 127) + (lax.shift_right_logical(c, 10) & 3) * 128)
    onehot[t] = hot
    return hot


def grouped(body, state, tick):
    def group(g, state):
        tick(g)
        for n in range(GROUP):
            state = body(g * GROUP + n, state)
        return state

    return lax.fori_loop(0, PAIRS // GROUP, group, state)


def project(s, flat, onehot, line, values, build, tick):
    lane = lax.broadcasted_iota(I32, (8, 128), 1)

    def body(u, state):
        columns, largest = state
        t = s * PAIRS + u
        if build is None:
            hot = onehot[t]
        else:
            hot = build(s, u)
        g = jnp.dot(flat[...], hot, preferred_element_type=F32)
        mask = lax.broadcasted_iota(I32, (STRIP, WIDE), 0) == line[t]
        p = values[t]
        if build is not None:
            for n in range(6):
                largest = jnp.maximum(largest, jnp.abs(p[:, n * 128 : (n + 1) * 128]))
        out = []
        for o in range(ORB):
            both = (
                g[o * STRIP : (o + 1) * STRIP]
                + g[(ORB + o) * STRIP : (ORB + o + 1) * STRIP]
            )
            q = p * jnp.sum(jnp.where(mask, both, 0.0), axis=0, keepdims=True)
            first = jnp.sum(q[:, :SUPP], axis=1, keepdims=True)
            second = jnp.sum(q[:, SUPP:], axis=1, keepdims=True)
            column = jnp.where(lane == 2 * u, first, columns[o])
            out.append(jnp.where(lane == 2 * u + 1, second, column))
        return tuple(out), largest

    start = tuple(jnp.zeros((8, 128), F32) for _ in range(ORB)), jnp.zeros((8, 128), F32)
    return grouped(body, start, tick)


def place(s, weights, onehot, line, values, total, tick):
    lane = lax.broadcasted_iota(I32, (8, 128), 1)

    def body(u, carry):
        t = s * PAIRS + u
        mask = lax.broadcasted_iota(I32, (STRIP, WIDE), 0) == line[t]
        p = values[t]
        firsts, seconds = [], []
        for o in range(ORB):
            w = weights[s, o * 8 : (o + 1) * 8, :]
            left = jnp.sum(jnp.where(lane == 2 * u, w, 0.0), axis=1, keepdims=True)
            right = jnp.sum(jnp.where(lane == 2 * u + 1, w, 0.0), axis=1, keepdims=True)
            spread = jnp.concatenate(
                [
                    jnp.sum(p[:, :SUPP] * left, axis=0, keepdims=True),
                    jnp.sum(p[:, SUPP:] * right, axis=0, keepdims=True),
                ],
                axis=1,
            )
            first, second = two_terms(spread)
            firsts.append(jnp.where(mask, first, 0.0))
            seconds.append(jnp.where(mask, second, 0.0))
        g = lax.dot_general(
            jnp.concatenate(firsts + seconds, axis=0).astype(F8),
            onehot[t],
            NT,
            preferred_element_type=F32,
        )
        total[s] += g[: ORB * STRIP] + g[ORB * STRIP :]
        return carry

    grouped(body, 0, tick)


def placed_planes(total, back, o, x):
    rows = slice(o * STRIP + 8 * x, o * STRIP + 8 * x + 8)
    return jnp.concatenate(
        [
            total[0, rows, q * 128 : (q + 1) * 128] * back[0][o]
            + total[1, rows, q * 128 : (q + 1) * 128] * back[1][o]
            for q in range(4)
        ],
        axis=0,
    )


def kernel(
    orbitals, potential, support, projectors, slot_rows, energies, panel,
    filtered, sums,
    onehot, line, values, flat, sent, halo_low, halo_high, table, got, weights, perm, own_slots,
    energy, local, degree_one, total, result, panel_raw, panel_wide, panel_lines, panel_here,
    ship, landed, spread_rows, gram,
    gram_out, gram_in, red, red_out, red_in,
    halo_send, halo_recv, coef_send, coef_recv, panel_send, panel_recv, panel_sem,
    ship_send, ship_recv, gram_send, gram_recv, red_send, red_recv, out_sem,
):
    band = lax.axis_index("band")
    dom = lax.axis_index("dom")
    right, left = lax.rem(dom + 1, PEERS), lax.rem(dom + PEERS - 1, PEERS)
    barrier = pltpu.get_barrier_semaphore()

    def greet(i, carry):
        pl.semaphore_signal(
            barrier, inc=1, device_id=(lax.rem(band + i, PEERS), dom), device_id_type=MESH
        )
        pl.semaphore_signal(
            barrier, inc=1, device_id=(band, lax.rem(dom + i, PEERS)), device_id_type=MESH
        )
        return carry

    lax.fori_loop(1, PEERS, greet, 0)

    fetch = pltpu.make_async_copy(panel, panel_raw, panel_sem)
    fetch.start()
    back_one = to_flat(orbitals, flat, sent.at[0])
    own_slots[...] = jnp.full((2, 8, 128), -1, I32)
    energy[...] = jnp.zeros((2, 8, 128), F32)
    for s, block in ((0, dom), (1, left)):
        own_slots[s, 0:1, 0:ATOMS] = slot_rows[0, s : s + 1, :]
        hit = lax.broadcasted_iota(I32, (128, 128), 0) == own_slots[s, 0:1, :]
        perm[s] = jnp.where(hit, 1.0, 0.0)
        energy[s, :, 0:ATOMS] = energies[block]

    fetch.wait()

    def widen(u, carry):
        for n in range(8):
            plane = u * 8 + n
            panel_wide[pl.ds(pl.multiple_of(plane * 32, 32), 32), :] = panel_raw[
                plane // 6, plane % 6
            ].astype(F32)
        return carry

    lax.fori_loop(0, PANEL_DEV * 6 // 8, widen, 0)
    pl.semaphore_wait(barrier, 2 * (PEERS - 1))

    def to_side(source, target, send, recv, side):
        return pltpu.make_async_remote_copy(
            src_ref=source, dst_ref=target, send_sem=send, recv_sem=recv,
            device_id=(band, side), device_id_type=MESH,
        )

    def halo_copies(d):
        return (
            to_side(sent.at[d], halo_low.at[d], halo_send.at[d, 0], halo_recv.at[d, 0], right),
            to_side(sent.at[d], halo_high.at[d], halo_send.at[d, 1], halo_recv.at[d, 1], left),
        )

    def coef_copy(d, s):
        return to_side(
            table.at[d, s], got.at[d, s], coef_send.at[d, s], coef_recv.at[d, s],
            left if s else right,
        )

    def panel_copy(i):
        peer = lax.rem(band + i, PEERS)
        return pltpu.make_async_remote_copy(
            src_ref=panel_lines.at[pl.ds(peer * CHUNK, CHUNK)],
            dst_ref=panel_here.at[:, pl.ds(pl.multiple_of(band * PANEL_DEV, PANEL_DEV), PANEL_DEV), :],
            send_sem=panel_send.at[i], recv_sem=panel_recv.at[i],
            device_id=(peer, dom), device_id_type=MESH,
        )

    def each(copy_of, action):
        def body(i, carry):
            getattr(copy_of(i), action)()
            return carry

        lax.fori_loop(1, PEERS, body, 0)

    for copy in halo_copies(0):
        copy.start()

    def send_panel(j):
        near = (j + 1) // 2
        i = near + (1 - j % 2) * (PEERS - 2 * near)
        peer = lax.rem(band + i, PEERS)
        for n in range(CHUNK):
            row = peer * CHUNK + n
            panel_lines[row] = panel_wide[pl.ds(row, PANEL_DEV, stride=ROWS), :].astype(BF16)
        panel_copy(i).start()

    steps = PAIRS // GROUP
    early = PEERS - 1 - 6 * steps
    for j in range(1, 1 + early):
        send_panel(j)

    def tick_of(stage):
        if stage < 6:
            return lambda g: send_panel(1 + early + stage * steps + g)
        return lambda g: None

    for n in range(CHUNK):
        row = band * CHUNK + n
        own = pl.ds(pl.multiple_of(band * PANEL_DEV, PANEL_DEV), PANEL_DEV)
        panel_here[n, own, :] = panel_wide[pl.ds(row, PANEL_DEV, stride=ROWS), :].astype(BF16)

    def build(s, u):
        return build_one(s, u, support, projectors, onehot, line, values)

    def apply(d, source, back, build, largest):
        found = []
        for n, s in enumerate((1, 0)):
            tick = tick_of(4 * d + n)
            columns, peaks = project(s, flat, onehot, line, values, build, tick)
            found.append(peaks)
            columns = jnp.concatenate([columns[o] * back[o] for o in range(ORB)], axis=0)
            table[d, s] = lax.dot_general(
                columns, perm[s], NT, precision=HIGHEST, preferred_element_type=F32
            )
            coef_copy(d, s).start()
        if largest is None:
            largest = jnp.max(jnp.maximum(found[0], found[1]), axis=1, keepdims=True)
        for copy in halo_copies(d):
            copy.wait_recv()
        local_part(source, halo_low.at[d], halo_high.at[d], potential, local)
        total[...] = jnp.zeros(total.shape, F32)
        scales = []
        for s in (0, 1):
            coef_copy(d, 1 - s).wait_recv()
            scaled = jnp.concatenate([energy[s]] * ORB, axis=0) * (table[d, s] + got[d, 1 - s])
            own = jnp.dot(scaled, perm[s], precision=HIGHEST, preferred_element_type=F32)
            scales.append([])
            for o in range(ORB):
                w = own[o * 8 : (o + 1) * 8, :]
                most = jnp.sum(jnp.abs(w) * largest, axis=0, keepdims=True)
                most = jnp.maximum(jnp.max(most, axis=1, keepdims=True), 1e-30)
                weights[s, o * 8 : (o + 1) * 8, :] = w * (TOP / most)
                scales[s].append(most * (1.0 / TOP))
            place(s, weights, onehot, line, values, total, tick_of(4 * d + 2 + s))
        return largest, scales

    largest, scales = apply(0, orbitals, back_one, build, None)
    for o in range(ORB):
        for x in range(6):
            degree_one[o, x] = (local[o, x] + placed_planes(total, scales, o, x)) * (
                1.0 / half_width
            )
    back_two = to_flat(degree_one, flat, sent.at[1])
    for copy in halo_copies(1):
        copy.start()

    largest, scales = apply(1, degree_one, back_two, None, largest)
    for o in range(ORB):
        for x in range(6):
            new = (local[o, x] + placed_planes(total, scales, o, x)) * (
                2.0 / half_width
            ) - orbitals[o, x]
            degree_one[o, x] = new
            result[o, x * 32 : (x + 1) * 32, :] = new
    write = pltpu.make_async_copy(degree_one, filtered, out_sem)
    write.start()

    for c in range(PEERS):
        for o in range(ORB):
            spread_rows[c * ORB * CHUNK + o * CHUNK : c * ORB * CHUNK + (o + 1) * CHUNK, :] = result[
                o, c * CHUNK : (c + 1) * CHUNK, :
            ]
        ship[c] = spread_rows[c * ORB * CHUNK : (c + 1) * ORB * CHUNK, :].astype(BF16)

    def ship_copy(i):
        peer = lax.rem(band + i, PEERS)
        return pltpu.make_async_remote_copy(
            src_ref=ship.at[peer], dst_ref=landed.at[band],
            send_sem=ship_send.at[i], recv_sem=ship_recv.at[i],
            device_id=(peer, dom), device_id_type=MESH,
        )

    each(ship_copy, "start")
    landed[band] = ship[band]
    each(panel_copy, "wait_recv")
    each(ship_copy, "wait_recv")

    for c in range(PEERS):
        spread_rows[c * ORB * CHUNK : (c + 1) * ORB * CHUNK, :] = landed[c].astype(F32)
    products = jnp.zeros((ORB * PEERS, PEERS * PANEL_DEV), F32)
    for k in range(0, CHUNK, 2):
        lines = [
            jnp.concatenate(
                [
                    spread_rows[pl.ds(o * CHUNK + n, PEERS, stride=ORB * CHUNK), :]
                    for o in range(ORB)
                ],
                axis=0,
            )
            for n in (k, k + 1)
        ]
        products += lax.dot_general(
            jnp.concatenate(lines, axis=1).astype(BF16),
            jnp.concatenate([panel_here[k], panel_here[k + 1]], axis=1),
            NT,
            preferred_element_type=F32,
        )
    for n in range(4):
        gram[n] = products[:, n * 128 : (n + 1) * 128]

    for d in range(PEERS):
        for n in range(4):
            gram_out[
                d, (n // 2) * ORB : (n // 2) * ORB + ORB, (n % 2) * 128 : (n % 2) * 128 + 128
            ] = gram[n, pl.ds(d, ORB, stride=PEERS), :]

    def gram_copy(i):
        peer = lax.rem(dom + i, PEERS)
        return pltpu.make_async_remote_copy(
            src_ref=gram_out.at[peer], dst_ref=gram_in.at[dom],
            send_sem=gram_send.at[i], recv_sem=gram_recv.at[i],
            device_id=(band, peer), device_id_type=MESH,
        )

    each(gram_copy, "start")
    gram_in[dom] = gram_out[dom]
    each(gram_copy, "wait_recv")
    red[...] = jnp.sum(gram_in[...], axis=0)
    red_out[...] = jnp.zeros(red_out.shape, F32)
    for b in range(PEERS):
        half, at = b // 8, (b % 8) * PANEL_DEV
        red_out[b, 0:ORB, 0:PANEL_DEV] = red[half * ORB : (half + 1) * ORB, at : at + PANEL_DEV]

    def red_copy(i):
        peer = lax.rem(band + i, PEERS)
        return pltpu.make_async_remote_copy(
            src_ref=red_out.at[peer], dst_ref=red_in.at[band],
            send_sem=red_send.at[i], recv_sem=red_recv.at[i],
            device_id=(peer, dom), device_id_type=MESH,
        )

    each(red_copy, "start")
    red_in[band] = red_out[band]
    each(red_copy, "wait_recv")
    sums[...] = jnp.sum(red_in[...], axis=0)

    write.wait()
    for d in range(2):
        for copy in halo_copies(d):
            copy.wait_send()
        for s in range(2):
            coef_copy(d, s).wait_send()
    for copy_of in (panel_copy, ship_copy, gram_copy, red_copy):
        each(copy_of, "wait_send")


def finish(raw, sums, filtered, correlation):
    filtered[...] = raw[...]
    correlation[...] = sums[0:ORB, 0:PANEL_DEV] * float(PEERS * ROWS * 128) ** (-0.5)


def per_device(orbitals, potential, support, projectors, slot_rows, energies, panel_orbitals):
    vmem = pl.BlockSpec(memory_space=pltpu.VMEM)
    anywhere = pl.BlockSpec(memory_space=pl.ANY)
    dma = pltpu.SemaphoreType.DMA
    raw, sums = pl.pallas_call(
        kernel,
        out_shape=(
            jax.ShapeDtypeStruct((ORB, 6, 32, 128), F32),
            jax.ShapeDtypeStruct((8, 128), F32),
        ),
        in_specs=[vmem] * 6 + [anywhere],
        out_specs=(anywhere, vmem),
        scratch_shapes=[
            pltpu.VMEM((2 * PAIRS, 512, WIDE), F8),
            pltpu.VMEM((2 * PAIRS, 1, WIDE), I32),
            pltpu.VMEM((2 * PAIRS, 8, WIDE), F32),
            pltpu.VMEM((2 * ORB * STRIP, 512), F8),
            pltpu.VMEM((2, ORB, 6, 32, 128), BF16),
            pltpu.VMEM((2, ORB, 6, 32, 128), BF16),
            pltpu.VMEM((2, ORB, 6, 32, 128), BF16),
            pltpu.VMEM((2, 2, ORB * 8, 128), F32),
            pltpu.VMEM((2, 2, ORB * 8, 128), F32),
            pltpu.VMEM((2, ORB * 8, 128), F32),
            pltpu.VMEM((2, 128, 128), F32),
            pltpu.VMEM((2, 8, 128), I32),
            pltpu.VMEM((2, 8, 128), F32),
            pltpu.VMEM((ORB, 6, 32, 128), F32),
            pltpu.VMEM((ORB, 6, 32, 128), F32),
            pltpu.VMEM((2, ORB * STRIP, 512), F32),
            pltpu.VMEM((ORB, ROWS, 128), F32),
            pltpu.VMEM((PANEL_DEV, 6, 32, 128), BF16),
            pltpu.VMEM((PANEL_DEV * ROWS, 128), F32),
            pltpu.VMEM((ROWS, PANEL_DEV, 128), BF16),
            pltpu.VMEM((CHUNK, PEERS * PANEL_DEV, 128), BF16),
            pltpu.VMEM((PEERS, ORB * CHUNK, 128), BF16),
            pltpu.VMEM((PEERS, ORB * CHUNK, 128), BF16),
            pltpu.VMEM((PEERS * ORB * CHUNK, 128), F32),
            pltpu.VMEM((4, ORB * PEERS, 128), F32),
            pltpu.VMEM((PEERS, 2 * ORB, 256), F32),
            pltpu.VMEM((PEERS, 2 * ORB, 256), F32),
            pltpu.VMEM((2 * ORB, 256), F32),
            pltpu.VMEM((PEERS, 8, 128), F32),
            pltpu.VMEM((PEERS, 8, 128), F32),
            dma((2, 2)), dma((2, 2)),
            dma((2, 2)), dma((2, 2)),
            dma((PEERS,)), dma((PEERS,)), dma,
            dma((PEERS,)), dma((PEERS,)),
            dma((PEERS,)), dma((PEERS,)),
            dma((PEERS,)), dma((PEERS,)),
            dma,
        ],
        compiler_params=pltpu.CompilerParams(
            collective_id=0, has_side_effects=True, vmem_limit_bytes=60 * 2**20
        ),
    )(
        orbitals,
        potential,
        support,
        projectors,
        slot_rows,
        energies.transpose(0, 2, 1),
        panel_orbitals,
    )
    return pl.pallas_call(
        finish,
        out_shape=(
            jax.ShapeDtypeStruct((ORB, 6, 32, 128), F32),
            jax.ShapeDtypeStruct((ORB, PANEL_DEV), F32),
        ),
        in_specs=[vmem] * 2,
        out_specs=(vmem, vmem),
    )(raw, sums)


def solution(mesh):
    return jax.shard_map(
        per_device,
        mesh=mesh,
        in_specs=(
            P("band", "dom", None, None),
            P("dom", None, None),
            P("dom", None, None, None),
            P("dom", None, None, None, None),
            P("dom", None, None),
            P(),
            P("band", "dom", None, None),
        ),
        out_specs=(P("band", "dom", None, None), P("dom", "band")),
        check_vma=False,
    )
```

```python
import math

import jax
import jax.numpy as jnp
from jax import lax
from jax.experimental import pallas as pl
from jax.experimental.pallas import tpu as pltpu
from jax.sharding import PartitionSpec as P

center_shift = 7.5
half_width = 6.5

MESH = pl.DeviceIdType.MESH
I32, F32, BF16, F8 = jnp.int32, jnp.float32, jnp.bfloat16, jnp.float8_e4m3fn

ORB = 4
ROWS = 192
STRIP = 48
TOP = 224.0
GROUP = 12
PEERS = 16
ATOMS = 48
SUPP = 384
PAIRS = 24
WIDE = 2 * SUPP
CHUNK = ROWS // PEERS
PANEL_DEV = 32
NT = (((1,), (1,)), ((), ()))
NN = (((1,), (0,)), ((), ()))


def tapered_stencil():
    unscaled = [
        2.0
        * (-1.0) ** (reach + 1)
        * math.sin(math.pi * reach / 8.0)
        / (math.pi * reach / 8.0 * reach * reach)
        for reach in range(1, 7)
    ]
    moment = sum((reach * reach * unscaled[reach - 1] for reach in range(1, 7)))
    side_terms = [neighbour_term / moment for neighbour_term in unscaled]
    return tuple([-2.0 * sum(side_terms)] + side_terms)


def local_part(source, low, high, potential, target):
    stencil = tapered_stencil()

    def one(o, carry):
        planes = [low[o, x].astype(F32) for x in range(6)]
        planes += [source[o, x] for x in range(6)]
        planes += [high[o, x].astype(F32) for x in range(6)]
        for x in range(6):
            f = planes[6 + x]
            total = (potential[x] + (-1.5 * stencil[0] - center_shift)) * f
            for k in range(1, 7):
                around = planes[6 + x + k] + planes[6 + x - k]
                around += pltpu.roll(f, k, 0) + pltpu.roll(f, 32 - k, 0)
                around += pltpu.roll(f, k, 1) + pltpu.roll(f, 128 - k, 1)
                total += (-0.5 * stencil[k]) * around
            target[o, x] = total
        return carry

    lax.fori_loop(0, ORB, one, 0)


def two_terms(x):
    first = x.astype(F8).astype(F32)
    return first, x - first


def peak(x):
    return jnp.max(jnp.max(jnp.abs(x), axis=0, keepdims=True), axis=1, keepdims=True)


def to_flat(source, flat, sent):
    back, terms = [], []
    for o in range(ORB):
        f = source[o]
        sent[o] = f.astype(BF16)
        top = jnp.maximum(peak(f.reshape(ROWS, 128)), 1e-30)
        back.append(top * (1.0 / TOP))
        terms.append(two_terms(f * (TOP / top)[None]))
    for n in range(2):
        for q in range(4):
            strip = [t[n][:, 8 * q : 8 * q + 8, :].reshape(STRIP, 128) for t in terms]
            flat[n * ORB * STRIP : (n + 1) * ORB * STRIP, q * 128 : (q + 1) * 128] = (
                jnp.concatenate(strip, axis=0).astype(F8)
            )
    return back


def onehot_of(spot):
    wide = jnp.broadcast_to(spot, (16, WIDE))
    upper = wide >= 256
    low = jnp.where(upper, -1.0, wide.astype(F32)).astype(BF16)
    high = jnp.where(upper, (wide - 256).astype(F32), -1.0).astype(BF16)
    count = lax.broadcasted_iota(I32, (16, WIDE), 0).astype(F32).astype(BF16)
    one, zero = jnp.array(1, BF16), jnp.array(0, BF16)
    parts = [
        jnp.where(count + jnp.array(16.0 * k, BF16) == side, one, zero)
        for side in (low, high)
        for k in range(16)
    ]
    return jnp.concatenate(parts, axis=0).astype(F8)


def build_one(s, u, support, projectors, onehot, line, values):
    t = s * PAIRS + u
    c = jnp.concatenate(
        [support[0, s, pl.ds(2 * u, 1), :], support[0, s, pl.ds(2 * u + 1, 1), :]], axis=1
    )
    values[t] = jnp.concatenate([projectors[0, s, 2 * u], projectors[0, s, 2 * u + 1]], axis=1)
    line[t] = lax.shift_right_logical(c, 12) * 8 + (lax.shift_right_logical(c, 7) & 7)
    hot = onehot_of((c & 127) + (lax.shift_right_logical(c, 10) & 3) * 128)
    onehot[t] = hot
    return hot


def grouped(body, state, tick):
    def group(g, state):
        tick(g)
        for n in range(GROUP):
            state = body(g * GROUP + n, state)
        return state

    return lax.fori_loop(0, PAIRS // GROUP, group, state)


def project(s, flat, onehot, line, values, build, tick):
    lane = lax.broadcasted_iota(I32, (8, 128), 1)

    def body(u, state):
        columns, largest = state
        t = s * PAIRS + u
        if build is None:
            hot = onehot[t]
        else:
            hot = build(s, u)
        g = jnp.dot(flat[...], hot, preferred_element_type=F32)
        mask = lax.broadcasted_iota(I32, (STRIP, WIDE), 0) == line[t]
        p = values[t]
        if build is not None:
            for n in range(6):
                largest = jnp.maximum(largest, jnp.abs(p[:, n * 128 : (n + 1) * 128]))
        out = []
        for o in range(ORB):
            both = (
                g[o * STRIP : (o + 1) * STRIP]
                + g[(ORB + o) * STRIP : (ORB + o + 1) * STRIP]
            )
            q = p * jnp.sum(jnp.where(mask, both, 0.0), axis=0, keepdims=True)
            first = jnp.sum(q[:, :SUPP], axis=1, keepdims=True)
            second = jnp.sum(q[:, SUPP:], axis=1, keepdims=True)
            column = jnp.where(lane == 2 * u, first, columns[o])
            out.append(jnp.where(lane == 2 * u + 1, second, column))
        return tuple(out), largest

    start = tuple(jnp.zeros((8, 128), F32) for _ in range(ORB)), jnp.zeros((8, 128), F32)
    return grouped(body, start, tick)


def permuted(x, perm, dims):
    parts = []
    for n in range(3):
        parts.append(x.astype(BF16))
        x = x - parts[n].astype(F32)
    y = lax.dot_general(jnp.concatenate(parts, axis=0), perm, dims, preferred_element_type=F32)
    rows = x.shape[0]
    return y[:rows] + y[rows : 2 * rows] + y[2 * rows :]


def place(s, weights, onehot, line, values, total, tick):
    lane = lax.broadcasted_iota(I32, (8, 128), 1)

    def body(u, carry):
        t = s * PAIRS + u
        mask = lax.broadcasted_iota(I32, (STRIP, WIDE), 0) == line[t]
        p = values[t]
        firsts, seconds = [], []
        for o in range(ORB):
            w = weights[s, o * 8 : (o + 1) * 8, :]
            left = jnp.sum(jnp.where(lane == 2 * u, w, 0.0), axis=1, keepdims=True)
            right = jnp.sum(jnp.where(lane == 2 * u + 1, w, 0.0), axis=1, keepdims=True)
            spread = jnp.concatenate(
                [
                    jnp.sum(p[:, :SUPP] * left, axis=0, keepdims=True),
                    jnp.sum(p[:, SUPP:] * right, axis=0, keepdims=True),
                ],
                axis=1,
            )
            first, second = two_terms(spread)
            firsts.append(jnp.where(mask, first, 0.0))
            seconds.append(jnp.where(mask, second, 0.0))
        g = lax.dot_general(
            jnp.concatenate(firsts + seconds, axis=0).astype(F8),
            onehot[t],
            NT,
            preferred_element_type=F32,
        )
        total[s] += g[: ORB * STRIP] + g[ORB * STRIP :]
        return carry

    grouped(body, 0, tick)


def placed_planes(total, back, o, x):
    rows = slice(o * STRIP + 8 * x, o * STRIP + 8 * x + 8)
    return jnp.concatenate(
        [
            total[0, rows, q * 128 : (q + 1) * 128] * back[0][o]
            + total[1, rows, q * 128 : (q + 1) * 128] * back[1][o]
            for q in range(4)
        ],
        axis=0,
    )


def kernel(
    orbitals, potential, support, projectors, slot_rows, energies, panel,
    filtered, sums,
    onehot, line, values, flat, sent, halo_low, halo_high, table, got, weights, perm, own_slots,
    energy, local, degree_one, total, result, panel_raw, panel_lines, panel_here,
    ship, landed, spread_rows, gram,
    gram_out, gram_in, red, red_out, red_in,
    halo_send, halo_recv, coef_send, coef_recv, panel_send, panel_recv, panel_sem,
    ship_send, ship_recv, gram_send, gram_recv, red_send, red_recv, out_sem,
):
    band = lax.axis_index("band")
    dom = lax.axis_index("dom")
    right, left = lax.rem(dom + 1, PEERS), lax.rem(dom + PEERS - 1, PEERS)
    barrier = pltpu.get_barrier_semaphore()

    def greet(i, carry):
        pl.semaphore_signal(
            barrier, inc=1, device_id=(lax.rem(band + i, PEERS), dom), device_id_type=MESH
        )
        pl.semaphore_signal(
            barrier, inc=1, device_id=(band, lax.rem(dom + i, PEERS)), device_id_type=MESH
        )
        return carry

    lax.fori_loop(1, PEERS, greet, 0)

    fetch = pltpu.make_async_copy(panel, panel_raw, panel_sem)
    fetch.start()
    back_one = to_flat(orbitals, flat, sent.at[0])
    own_slots[...] = jnp.full((2, 8, 128), -1, I32)
    energy[...] = jnp.zeros((2, 8, 128), F32)
    for s, block in ((0, dom), (1, left)):
        own_slots[s, 0:1, 0:ATOMS] = slot_rows[0, s : s + 1, :]
        hit = lax.broadcasted_iota(I32, (128, 128), 0) == own_slots[s, 0:1, :]
        perm[s] = jnp.where(hit, 1.0, 0.0).astype(BF16)
        energy[s, :, 0:ATOMS] = energies[block]

    fetch.wait()

    def turn(x, carry):
        for y in (0, 16):
            lines = jnp.swapaxes(panel_raw[:, x, y : y + 16, :], 0, 1)
            panel_lines[pl.ds(pl.multiple_of(x * 32 + y, 16), 16)] = lines
        return carry

    lax.fori_loop(0, 6, turn, 0)
    pl.semaphore_wait(barrier, 2 * (PEERS - 1))

    def to_side(source, target, send, recv, side):
        return pltpu.make_async_remote_copy(
            src_ref=source, dst_ref=target, send_sem=send, recv_sem=recv,
            device_id=(band, side), device_id_type=MESH,
        )

    def halo_copies(d):
        return (
            to_side(sent.at[d], halo_low.at[d], halo_send.at[d, 0], halo_recv.at[d, 0], right),
            to_side(sent.at[d], halo_high.at[d], halo_send.at[d, 1], halo_recv.at[d, 1], left),
        )

    def coef_copy(d, s):
        return to_side(
            table.at[d, s], got.at[d, s], coef_send.at[d, s], coef_recv.at[d, s],
            left if s else right,
        )

    def panel_copy(i):
        peer = lax.rem(band + i, PEERS)
        return pltpu.make_async_remote_copy(
            src_ref=panel_lines.at[pl.ds(peer * CHUNK, CHUNK)],
            dst_ref=panel_here.at[:, pl.ds(pl.multiple_of(band * PANEL_DEV, PANEL_DEV), PANEL_DEV), :],
            send_sem=panel_send.at[i], recv_sem=panel_recv.at[i],
            device_id=(peer, dom), device_id_type=MESH,
        )

    def each(copy_of, action):
        def body(i, carry):
            getattr(copy_of(i), action)()
            return carry

        lax.fori_loop(1, PEERS, body, 0)

    for copy in halo_copies(0):
        copy.start()

    def send_panel(j):
        near = (j + 1) // 2
        i = near + (1 - j % 2) * (PEERS - 2 * near)
        panel_copy(i).start()

    steps = PAIRS // GROUP
    early = PEERS - 1 - 6 * steps
    for j in range(1, 1 + early):
        send_panel(j)

    def tick_of(stage):
        if stage < 6:
            return lambda g: send_panel(1 + early + stage * steps + g)
        return lambda g: None

    for n in range(CHUNK):
        own = pl.ds(pl.multiple_of(band * PANEL_DEV, PANEL_DEV), PANEL_DEV)
        panel_here[n, own, :] = panel_lines[band * CHUNK + n]

    def build(s, u):
        return build_one(s, u, support, projectors, onehot, line, values)

    def apply(d, source, back, build, largest):
        found = []
        for n, s in enumerate((1, 0)):
            tick = tick_of(4 * d + n)
            columns, peaks = project(s, flat, onehot, line, values, build, tick)
            found.append(peaks)
            columns = jnp.concatenate([columns[o] * back[o] for o in range(ORB)], axis=0)
            table[d, s] = permuted(columns, perm[s], NT)
            coef_copy(d, s).start()
        if largest is None:
            largest = jnp.max(jnp.maximum(found[0], found[1]), axis=1, keepdims=True)
        for copy in halo_copies(d):
            copy.wait_recv()
        local_part(source, halo_low.at[d], halo_high.at[d], potential, local)
        total[...] = jnp.zeros(total.shape, F32)
        scales = []
        for s in (0, 1):
            coef_copy(d, 1 - s).wait_recv()
            scaled = jnp.concatenate([energy[s]] * ORB, axis=0) * (table[d, s] + got[d, 1 - s])
            own = permuted(scaled, perm[s], NN)
            scales.append([])
            for o in range(ORB):
                w = own[o * 8 : (o + 1) * 8, :]
                most = jnp.sum(jnp.abs(w) * largest, axis=0, keepdims=True)
                most = jnp.maximum(jnp.max(most, axis=1, keepdims=True), 1e-30)
                weights[s, o * 8 : (o + 1) * 8, :] = w * (TOP / most)
                scales[s].append(most * (1.0 / TOP))
            place(s, weights, onehot, line, values, total, tick_of(4 * d + 2 + s))
        return largest, scales

    largest, scales = apply(0, orbitals, back_one, build, None)
    for o in range(ORB):
        for x in range(6):
            degree_one[o, x] = (local[o, x] + placed_planes(total, scales, o, x)) * (
                1.0 / half_width
            )
    back_two = to_flat(degree_one, flat, sent.at[1])
    for copy in halo_copies(1):
        copy.start()

    largest, scales = apply(1, degree_one, back_two, None, largest)
    for o in range(ORB):
        for x in range(6):
            new = (local[o, x] + placed_planes(total, scales, o, x)) * (
                2.0 / half_width
            ) - orbitals[o, x]
            degree_one[o, x] = new
            result[o, x * 32 : (x + 1) * 32, :] = new
    write = pltpu.make_async_copy(degree_one, filtered, out_sem)
    write.start()

    for c in range(PEERS):
        for o in range(ORB):
            spread_rows[c * ORB * CHUNK + o * CHUNK : c * ORB * CHUNK + (o + 1) * CHUNK, :] = result[
                o, c * CHUNK : (c + 1) * CHUNK, :
            ]
        ship[c] = spread_rows[c * ORB * CHUNK : (c + 1) * ORB * CHUNK, :].astype(BF16)

    def ship_copy(i):
        peer = lax.rem(band + i, PEERS)
        return pltpu.make_async_remote_copy(
            src_ref=ship.at[peer], dst_ref=landed.at[band],
            send_sem=ship_send.at[i], recv_sem=ship_recv.at[i],
            device_id=(peer, dom), device_id_type=MESH,
        )

    each(ship_copy, "start")
    landed[band] = ship[band]
    each(panel_copy, "wait_recv")
    each(ship_copy, "wait_recv")

    for c in range(PEERS):
        spread_rows[c * ORB * CHUNK : (c + 1) * ORB * CHUNK, :] = landed[c].astype(F32)
    products = jnp.zeros((ORB * PEERS, PEERS * PANEL_DEV), F32)
    for k in range(0, CHUNK, 2):
        lines = [
            jnp.concatenate(
                [
                    spread_rows[pl.ds(o * CHUNK + n, PEERS, stride=ORB * CHUNK), :]
                    for o in range(ORB)
                ],
                axis=0,
            )
            for n in (k, k + 1)
        ]
        products += lax.dot_general(
            jnp.concatenate(lines, axis=1).astype(BF16),
            jnp.concatenate([panel_here[k], panel_here[k + 1]], axis=1),
            NT,
            preferred_element_type=F32,
        )
    for n in range(4):
        gram[n] = products[:, n * 128 : (n + 1) * 128]

    for d in range(PEERS):
        for n in range(4):
            gram_out[
                d, (n // 2) * ORB : (n // 2) * ORB + ORB, (n % 2) * 128 : (n % 2) * 128 + 128
            ] = gram[n, pl.ds(d, ORB, stride=PEERS), :]

    def gram_copy(i):
        peer = lax.rem(dom + i, PEERS)
        return pltpu.make_async_remote_copy(
            src_ref=gram_out.at[peer], dst_ref=gram_in.at[dom],
            send_sem=gram_send.at[i], recv_sem=gram_recv.at[i],
            device_id=(band, peer), device_id_type=MESH,
        )

    each(gram_copy, "start")
    gram_in[dom] = gram_out[dom]
    each(gram_copy, "wait_recv")
    red[...] = jnp.sum(gram_in[...], axis=0)
    red_out[...] = jnp.zeros(red_out.shape, F32)
    for b in range(PEERS):
        half, at = b // 8, (b % 8) * PANEL_DEV
        red_out[b, 0:ORB, 0:PANEL_DEV] = red[half * ORB : (half + 1) * ORB, at : at + PANEL_DEV]

    def red_copy(i):
        peer = lax.rem(band + i, PEERS)
        return pltpu.make_async_remote_copy(
            src_ref=red_out.at[peer], dst_ref=red_in.at[band],
            send_sem=red_send.at[i], recv_sem=red_recv.at[i],
            device_id=(peer, dom), device_id_type=MESH,
        )

    each(red_copy, "start")
    red_in[band] = red_out[band]
    each(red_copy, "wait_recv")
    sums[...] = jnp.sum(red_in[...], axis=0)

    write.wait()
    for d in range(2):
        for copy in halo_copies(d):
            copy.wait_send()
        for s in range(2):
            coef_copy(d, s).wait_send()
    for copy_of in (panel_copy, ship_copy, gram_copy, red_copy):
        each(copy_of, "wait_send")


def finish(raw, sums, filtered, correlation):
    filtered[...] = raw[...]
    correlation[...] = sums[0:ORB, 0:PANEL_DEV] * float(PEERS * ROWS * 128) ** (-0.5)


def per_device(orbitals, potential, support, projectors, slot_rows, energies, panel_orbitals):
    vmem = pl.BlockSpec(memory_space=pltpu.VMEM)
    anywhere = pl.BlockSpec(memory_space=pl.ANY)
    dma = pltpu.SemaphoreType.DMA
    raw, sums = pl.pallas_call(
        kernel,
        out_shape=(
            jax.ShapeDtypeStruct((ORB, 6, 32, 128), F32),
            jax.ShapeDtypeStruct((8, 128), F32),
        ),
        in_specs=[vmem] * 6 + [anywhere],
        out_specs=(anywhere, vmem),
        scratch_shapes=[
            pltpu.VMEM((2 * PAIRS, 512, WIDE), F8),
            pltpu.VMEM((2 * PAIRS, 1, WIDE), I32),
            pltpu.VMEM((2 * PAIRS, 8, WIDE), F32),
            pltpu.VMEM((2 * ORB * STRIP, 512), F8),
            pltpu.VMEM((2, ORB, 6, 32, 128), BF16),
            pltpu.VMEM((2, ORB, 6, 32, 128), BF16),
            pltpu.VMEM((2, ORB, 6, 32, 128), BF16),
            pltpu.VMEM((2, 2, ORB * 8, 128), F32),
            pltpu.VMEM((2, 2, ORB * 8, 128), F32),
            pltpu.VMEM((2, ORB * 8, 128), F32),
            pltpu.VMEM((2, 128, 128), BF16),
            pltpu.VMEM((2, 8, 128), I32),
            pltpu.VMEM((2, 8, 128), F32),
            pltpu.VMEM((ORB, 6, 32, 128), F32),
            pltpu.VMEM((ORB, 6, 32, 128), F32),
            pltpu.VMEM((2, ORB * STRIP, 512), F32),
            pltpu.VMEM((ORB, ROWS, 128), F32),
            pltpu.VMEM((PANEL_DEV, 6, 32, 128), BF16),
            pltpu.VMEM((ROWS, PANEL_DEV, 128), BF16),
            pltpu.VMEM((CHUNK, PEERS * PANEL_DEV, 128), BF16),
            pltpu.VMEM((PEERS, ORB * CHUNK, 128), BF16),
            pltpu.VMEM((PEERS, ORB * CHUNK, 128), BF16),
            pltpu.VMEM((PEERS * ORB * CHUNK, 128), F32),
            pltpu.VMEM((4, ORB * PEERS, 128), F32),
            pltpu.VMEM((PEERS, 2 * ORB, 256), F32),
            pltpu.VMEM((PEERS, 2 * ORB, 256), F32),
            pltpu.VMEM((2 * ORB, 256), F32),
            pltpu.VMEM((PEERS, 8, 128), F32),
            pltpu.VMEM((PEERS, 8, 128), F32),
            dma((2, 2)), dma((2, 2)),
            dma((2, 2)), dma((2, 2)),
            dma((PEERS,)), dma((PEERS,)), dma,
            dma((PEERS,)), dma((PEERS,)),
            dma((PEERS,)), dma((PEERS,)),
            dma((PEERS,)), dma((PEERS,)),
            dma,
        ],
        compiler_params=pltpu.CompilerParams(
            collective_id=0, has_side_effects=True, vmem_limit_bytes=60 * 2**20
        ),
    )(
        orbitals,
        potential,
        support,
        projectors,
        slot_rows,
        energies.transpose(0, 2, 1),
        panel_orbitals,
    )
    return pl.pallas_call(
        finish,
        out_shape=(
            jax.ShapeDtypeStruct((ORB, 6, 32, 128), F32),
            jax.ShapeDtypeStruct((ORB, PANEL_DEV), F32),
        ),
        in_specs=[vmem] * 2,
        out_specs=(vmem, vmem),
    )(raw, sums)


def solution(mesh):
    return jax.shard_map(
        per_device,
        mesh=mesh,
        in_specs=(
            P("band", "dom", None, None),
            P("dom", None, None),
            P("dom", None, None, None),
            P("dom", None, None, None, None),
            P("dom", None, None),
            P(),
            P("band", "dom", None, None),
        ),
        out_specs=(P("band", "dom", None, None), P("dom", "band")),
        check_vma=False,
    )
```

```python
import math

import jax
import jax.numpy as jnp
from jax import lax
from jax.experimental import pallas as pl
from jax.experimental.pallas import tpu as pltpu
from jax.sharding import PartitionSpec as P

center_shift = 7.5
half_width = 6.5

MESH = pl.DeviceIdType.MESH
I32, F32, BF16, F8 = jnp.int32, jnp.float32, jnp.bfloat16, jnp.float8_e4m3fn

ORB = 4
ROWS = 192
STRIP = 48
TOP = 224.0
GROUP = 12
PEERS = 16
ATOMS = 48
SUPP = 384
PAIRS = 24
WIDE = 2 * SUPP
CHUNK = ROWS // PEERS
PANEL_DEV = 32
NT = (((1,), (1,)), ((), ()))
NN = (((1,), (0,)), ((), ()))


def tapered_stencil():
    unscaled = [
        2.0
        * (-1.0) ** (reach + 1)
        * math.sin(math.pi * reach / 8.0)
        / (math.pi * reach / 8.0 * reach * reach)
        for reach in range(1, 7)
    ]
    moment = sum((reach * reach * unscaled[reach - 1] for reach in range(1, 7)))
    side_terms = [neighbour_term / moment for neighbour_term in unscaled]
    return tuple([-2.0 * sum(side_terms)] + side_terms)


def local_part(o, source, low, high, potential, target):
    stencil = tapered_stencil()
    planes = [low[o, x].astype(F32) for x in range(6)]
    planes += [source[o, x] for x in range(6)]
    planes += [high[o, x].astype(F32) for x in range(6)]
    for x in range(6):
        f = planes[6 + x]
        total = (potential[x] + (-1.5 * stencil[0] - center_shift)) * f
        for k in range(1, 7):
            around = planes[6 + x + k] + planes[6 + x - k]
            around += pltpu.roll(f, k, 0) + pltpu.roll(f, 32 - k, 0)
            around += pltpu.roll(f, k, 1) + pltpu.roll(f, 128 - k, 1)
            total += (-0.5 * stencil[k]) * around
        target[o, x] = total


def two_terms(x):
    first = x.astype(F8).astype(F32)
    return first, x - first


def peak(x):
    return jnp.max(jnp.max(jnp.abs(x), axis=0, keepdims=True), axis=1, keepdims=True)


def to_flat(source, flat, sent):
    back, terms = [], []
    for o in range(ORB):
        f = source[o]
        sent[o] = f.astype(BF16)
        top = jnp.maximum(peak(f.reshape(ROWS, 128)), 1e-30)
        back.append(top * (1.0 / TOP))
        terms.append(two_terms(f * (TOP / top)[None]))
    for n in range(2):
        for q in range(4):
            strip = [t[n][:, 8 * q : 8 * q + 8, :].reshape(STRIP, 128) for t in terms]
            flat[n * ORB * STRIP : (n + 1) * ORB * STRIP, q * 128 : (q + 1) * 128] = (
                jnp.concatenate(strip, axis=0).astype(F8)
            )
    return back


def onehot_of(spot):
    wide = jnp.broadcast_to(spot, (16, WIDE))
    upper = wide >= 256
    low = jnp.where(upper, -1.0, wide.astype(F32)).astype(BF16)
    high = jnp.where(upper, (wide - 256).astype(F32), -1.0).astype(BF16)
    count = lax.broadcasted_iota(I32, (16, WIDE), 0).astype(F32).astype(BF16)
    one, zero = jnp.array(1, BF16), jnp.array(0, BF16)
    parts = [
        jnp.where(count + jnp.array(16.0 * k, BF16) == side, one, zero)
        for side in (low, high)
        for k in range(16)
    ]
    return jnp.concatenate(parts, axis=0).astype(F8)


def build_one(s, u, support, projectors, onehot, line, values):
    t = s * PAIRS + u
    c = jnp.concatenate(
        [support[0, s, pl.ds(2 * u, 1), :], support[0, s, pl.ds(2 * u + 1, 1), :]], axis=1
    )
    values[t] = jnp.concatenate([projectors[0, s, 2 * u], projectors[0, s, 2 * u + 1]], axis=1)
    line[t] = lax.shift_right_logical(c, 12) * 8 + (lax.shift_right_logical(c, 7) & 7)
    hot = onehot_of((c & 127) + (lax.shift_right_logical(c, 10) & 3) * 128)
    onehot[t] = hot
    return hot


def grouped(body, state, tick):
    def group(g, state):
        tick(g)
        for n in range(GROUP):
            state = body(g * GROUP + n, state)
        return state

    return lax.fori_loop(0, PAIRS // GROUP, group, state)


def project(s, flat, onehot, line, values, build, tick):
    lane = lax.broadcasted_iota(I32, (8, 128), 1)

    def body(u, state):
        columns, largest = state
        t = s * PAIRS + u
        if build is None:
            hot = onehot[t]
        else:
            hot = build(s, u)
        g = jnp.dot(flat[...], hot, preferred_element_type=F32)
        mask = lax.broadcasted_iota(I32, (STRIP, WIDE), 0) == line[t]
        p = values[t]
        if build is not None:
            for n in range(6):
                largest = jnp.maximum(largest, jnp.abs(p[:, n * 128 : (n + 1) * 128]))
        out = []
        for o in range(ORB):
            both = (
                g[o * STRIP : (o + 1) * STRIP]
                + g[(ORB + o) * STRIP : (ORB + o + 1) * STRIP]
            )
            q = p * jnp.sum(jnp.where(mask, both, 0.0), axis=0, keepdims=True)
            first = jnp.sum(q[:, :SUPP], axis=1, keepdims=True)
            second = jnp.sum(q[:, SUPP:], axis=1, keepdims=True)
            column = jnp.where(lane == 2 * u, first, columns[o])
            out.append(jnp.where(lane == 2 * u + 1, second, column))
        return tuple(out), largest

    start = tuple(jnp.zeros((8, 128), F32) for _ in range(ORB)), jnp.zeros((8, 128), F32)
    return grouped(body, start, tick)


def permuted(x, perm, dims):
    parts = []
    for n in range(3):
        parts.append(x.astype(BF16))
        x = x - parts[n].astype(F32)
    y = lax.dot_general(jnp.concatenate(parts, axis=0), perm, dims, preferred_element_type=F32)
    rows = x.shape[0]
    return y[:rows] + y[rows : 2 * rows] + y[2 * rows :]


def place(s, weights, onehot, line, values, total, tick):
    lane = lax.broadcasted_iota(I32, (8, 128), 1)

    def body(u, carry):
        t = s * PAIRS + u
        mask = lax.broadcasted_iota(I32, (STRIP, WIDE), 0) == line[t]
        p = values[t]
        firsts, seconds = [], []
        for o in range(ORB):
            w = weights[s, o * 8 : (o + 1) * 8, :]
            left = jnp.sum(jnp.where(lane == 2 * u, w, 0.0), axis=1, keepdims=True)
            right = jnp.sum(jnp.where(lane == 2 * u + 1, w, 0.0), axis=1, keepdims=True)
            spread = jnp.concatenate(
                [
                    jnp.sum(p[:, :SUPP] * left, axis=0, keepdims=True),
                    jnp.sum(p[:, SUPP:] * right, axis=0, keepdims=True),
                ],
                axis=1,
            )
            first, second = two_terms(spread)
            firsts.append(jnp.where(mask, first, 0.0))
            seconds.append(jnp.where(mask, second, 0.0))
        g = lax.dot_general(
            jnp.concatenate(firsts + seconds, axis=0).astype(F8),
            onehot[t],
            NT,
            preferred_element_type=F32,
        )
        total[s] += g[: ORB * STRIP] + g[ORB * STRIP :]
        return carry

    grouped(body, 0, tick)


def placed_planes(total, back, o, x):
    rows = slice(o * STRIP + 8 * x, o * STRIP + 8 * x + 8)
    return jnp.concatenate(
        [
            total[0, rows, q * 128 : (q + 1) * 128] * back[0][o]
            + total[1, rows, q * 128 : (q + 1) * 128] * back[1][o]
            for q in range(4)
        ],
        axis=0,
    )


def kernel(
    orbitals, potential, support, projectors, slot_rows, energies, panel,
    filtered, sums,
    onehot, line, values, flat, sent, halo_low, halo_high, table, got, weights, perm, own_slots,
    energy, local, degree_one, total, result, panel_raw, panel_lines, panel_here,
    ship, landed, spread_rows, gram,
    gram_out, gram_in, red, red_out, red_in,
    halo_send, halo_recv, coef_send, coef_recv, panel_send, panel_recv, panel_sem,
    ship_send, ship_recv, gram_send, gram_recv, red_send, red_recv, out_sem,
):
    band = lax.axis_index("band")
    dom = lax.axis_index("dom")
    right, left = lax.rem(dom + 1, PEERS), lax.rem(dom + PEERS - 1, PEERS)
    barrier = pltpu.get_barrier_semaphore()

    def greet(i, carry):
        pl.semaphore_signal(
            barrier, inc=1, device_id=(lax.rem(band + i, PEERS), dom), device_id_type=MESH
        )
        pl.semaphore_signal(
            barrier, inc=1, device_id=(band, lax.rem(dom + i, PEERS)), device_id_type=MESH
        )
        return carry

    lax.fori_loop(1, PEERS, greet, 0)

    fetch = pltpu.make_async_copy(panel, panel_raw, panel_sem)
    fetch.start()
    back_one = to_flat(orbitals, flat, sent.at[0])
    own_slots[...] = jnp.full((2, 8, 128), -1, I32)
    energy[...] = jnp.zeros((2, 8, 128), F32)
    for s, block in ((0, dom), (1, left)):
        own_slots[s, 0:1, 0:ATOMS] = slot_rows[0, s : s + 1, :]
        hit = lax.broadcasted_iota(I32, (128, 128), 0) == own_slots[s, 0:1, :]
        perm[s] = jnp.where(hit, 1.0, 0.0).astype(BF16)
        energy[s, :, 0:ATOMS] = energies[block]

    fetch.wait()

    def turn(x, carry):
        for y in (0, 16):
            lines = jnp.swapaxes(panel_raw[:, x, y : y + 16, :], 0, 1)
            panel_lines[pl.ds(pl.multiple_of(x * 32 + y, 16), 16)] = lines
        return carry

    lax.fori_loop(0, 6, turn, 0)
    pl.semaphore_wait(barrier, 2 * (PEERS - 1))

    def to_side(source, target, send, recv, side):
        return pltpu.make_async_remote_copy(
            src_ref=source, dst_ref=target, send_sem=send, recv_sem=recv,
            device_id=(band, side), device_id_type=MESH,
        )

    def halo_copies(d):
        return (
            to_side(sent.at[d], halo_low.at[d], halo_send.at[d, 0], halo_recv.at[d, 0], right),
            to_side(sent.at[d], halo_high.at[d], halo_send.at[d, 1], halo_recv.at[d, 1], left),
        )

    def coef_copy(d, s):
        return to_side(
            table.at[d, s], got.at[d, s], coef_send.at[d, s], coef_recv.at[d, s],
            left if s else right,
        )

    def panel_copy(i):
        peer = lax.rem(band + i, PEERS)
        return pltpu.make_async_remote_copy(
            src_ref=panel_lines.at[pl.ds(peer * CHUNK, CHUNK)],
            dst_ref=panel_here.at[:, pl.ds(pl.multiple_of(band * PANEL_DEV, PANEL_DEV), PANEL_DEV), :],
            send_sem=panel_send.at[i], recv_sem=panel_recv.at[i],
            device_id=(peer, dom), device_id_type=MESH,
        )

    def each(copy_of, action):
        def body(i, carry):
            getattr(copy_of(i), action)()
            return carry

        lax.fori_loop(1, PEERS, body, 0)

    def far_first(copy_of, order):
        for i in order:
            copy_of(i).start()

    along_band = (4, 12, 3, 5, 11, 13, 2, 6, 10, 14, 1, 7, 9, 15, 8)
    along_dom = (8, 7, 9, 6, 10, 5, 11, 4, 12, 3, 13, 2, 14, 1, 15)
    for copy in halo_copies(0):
        copy.start()

    def send_panel(j):
        near = (j + 1) // 2
        i = near + (1 - j % 2) * (PEERS - 2 * near)
        panel_copy(i).start()

    steps = PAIRS // GROUP
    early = PEERS - 1 - 6 * steps
    for j in range(1, 1 + early):
        send_panel(j)

    def tick_of(stage):
        if stage < 6:
            return lambda g: send_panel(1 + early + stage * steps + g)
        return lambda g: None

    for n in range(CHUNK):
        own = pl.ds(pl.multiple_of(band * PANEL_DEV, PANEL_DEV), PANEL_DEV)
        panel_here[n, own, :] = panel_lines[band * CHUNK + n]

    def build(s, u):
        return build_one(s, u, support, projectors, onehot, line, values)

    def apply(d, source, back, build, largest):
        found = []
        for n, s in enumerate((1, 0)):
            tick = tick_of(4 * d + n)
            columns, peaks = project(s, flat, onehot, line, values, build, tick)
            found.append(peaks)
            columns = jnp.concatenate([columns[o] * back[o] for o in range(ORB)], axis=0)
            table[d, s] = permuted(columns, perm[s], NT)
            coef_copy(d, s).start()
        if largest is None:
            largest = jnp.max(jnp.maximum(found[0], found[1]), axis=1, keepdims=True)
        for copy in halo_copies(d):
            copy.wait_recv()
        total[...] = jnp.zeros(total.shape, F32)
        scales = []

        def beside(s):
            send = tick_of(4 * d + 2 + s)

            def tick(g):
                send(g)
                for n in range(ORB // 2 // steps):
                    o = s * (ORB // 2) + g * (ORB // 2 // steps) + n
                    local_part(o, source, halo_low.at[d], halo_high.at[d], potential, local)

            return tick

        for s in (0, 1):
            coef_copy(d, 1 - s).wait_recv()
            scaled = jnp.concatenate([energy[s]] * ORB, axis=0) * (table[d, s] + got[d, 1 - s])
            own = permuted(scaled, perm[s], NN)
            scales.append([])
            for o in range(ORB):
                w = own[o * 8 : (o + 1) * 8, :]
                most = jnp.sum(jnp.abs(w) * largest, axis=0, keepdims=True)
                most = jnp.maximum(jnp.max(most, axis=1, keepdims=True), 1e-30)
                weights[s, o * 8 : (o + 1) * 8, :] = w * (TOP / most)
                scales[s].append(most * (1.0 / TOP))
            place(s, weights, onehot, line, values, total, beside(s))
        return largest, scales

    largest, scales = apply(0, orbitals, back_one, build, None)
    for o in range(ORB):
        for x in range(6):
            degree_one[o, x] = (local[o, x] + placed_planes(total, scales, o, x)) * (
                1.0 / half_width
            )
    back_two = to_flat(degree_one, flat, sent.at[1])
    for copy in halo_copies(1):
        copy.start()

    largest, scales = apply(1, degree_one, back_two, None, largest)
    for o in range(ORB):
        for x in range(6):
            new = (local[o, x] + placed_planes(total, scales, o, x)) * (
                2.0 / half_width
            ) - orbitals[o, x]
            degree_one[o, x] = new
            result[o, x * 32 : (x + 1) * 32, :] = new
    write = pltpu.make_async_copy(degree_one, filtered, out_sem)
    write.start()

    for c in range(PEERS):
        for o in range(ORB):
            spread_rows[c * ORB * CHUNK + o * CHUNK : c * ORB * CHUNK + (o + 1) * CHUNK, :] = result[
                o, c * CHUNK : (c + 1) * CHUNK, :
            ]
        ship[c] = spread_rows[c * ORB * CHUNK : (c + 1) * ORB * CHUNK, :].astype(BF16)

    def ship_copy(i):
        peer = lax.rem(band + i, PEERS)
        return pltpu.make_async_remote_copy(
            src_ref=ship.at[peer], dst_ref=landed.at[band],
            send_sem=ship_send.at[i], recv_sem=ship_recv.at[i],
            device_id=(peer, dom), device_id_type=MESH,
        )

    far_first(ship_copy, along_band)
    landed[band] = ship[band]
    each(panel_copy, "wait_recv")
    each(ship_copy, "wait_recv")

    for c in range(PEERS):
        spread_rows[c * ORB * CHUNK : (c + 1) * ORB * CHUNK, :] = landed[c].astype(F32)
    products = jnp.zeros((ORB * PEERS, PEERS * PANEL_DEV), F32)
    for k in range(0, CHUNK, 2):
        lines = [
            jnp.concatenate(
                [
                    spread_rows[pl.ds(o * CHUNK + n, PEERS, stride=ORB * CHUNK), :]
                    for o in range(ORB)
                ],
                axis=0,
            )
            for n in (k, k + 1)
        ]
        products += lax.dot_general(
            jnp.concatenate(lines, axis=1).astype(BF16),
            jnp.concatenate([panel_here[k], panel_here[k + 1]], axis=1),
            NT,
            preferred_element_type=F32,
        )
    for n in range(4):
        gram[n] = products[:, n * 128 : (n + 1) * 128]

    for d in range(PEERS):
        for n in range(4):
            gram_out[
                d, (n // 2) * ORB : (n // 2) * ORB + ORB, (n % 2) * 128 : (n % 2) * 128 + 128
            ] = gram[n, pl.ds(d, ORB, stride=PEERS), :]

    def gram_copy(i):
        peer = lax.rem(dom + i, PEERS)
        return pltpu.make_async_remote_copy(
            src_ref=gram_out.at[peer], dst_ref=gram_in.at[dom],
            send_sem=gram_send.at[i], recv_sem=gram_recv.at[i],
            device_id=(band, peer), device_id_type=MESH,
        )

    far_first(gram_copy, along_dom)
    gram_in[dom] = gram_out[dom]
    each(gram_copy, "wait_recv")
    red[...] = jnp.sum(gram_in[...], axis=0)
    red_out[...] = jnp.zeros(red_out.shape, F32)
    for b in range(PEERS):
        half, at = b // 8, (b % 8) * PANEL_DEV
        red_out[b, 0:ORB, 0:PANEL_DEV] = red[half * ORB : (half + 1) * ORB, at : at + PANEL_DEV]

    def red_copy(i):
        peer = lax.rem(band + i, PEERS)
        return pltpu.make_async_remote_copy(
            src_ref=red_out.at[peer], dst_ref=red_in.at[band],
            send_sem=red_send.at[i], recv_sem=red_recv.at[i],
            device_id=(peer, dom), device_id_type=MESH,
        )

    far_first(red_copy, along_band)
    red_in[band] = red_out[band]
    write.wait()
    for d in range(2):
        for copy in halo_copies(d):
            copy.wait_send()
        for s in range(2):
            coef_copy(d, s).wait_send()
    for copy_of in (panel_copy, ship_copy, gram_copy):
        each(copy_of, "wait_send")
    each(red_copy, "wait_recv")
    sums[...] = jnp.sum(red_in[...], axis=0)
    each(red_copy, "wait_send")


def finish(raw, sums, filtered, correlation):
    filtered[...] = raw[...]
    correlation[...] = sums[0:ORB, 0:PANEL_DEV] * float(PEERS * ROWS * 128) ** (-0.5)


def per_device(orbitals, potential, support, projectors, slot_rows, energies, panel_orbitals):
    vmem = pl.BlockSpec(memory_space=pltpu.VMEM)
    anywhere = pl.BlockSpec(memory_space=pl.ANY)
    dma = pltpu.SemaphoreType.DMA
    raw, sums = pl.pallas_call(
        kernel,
        out_shape=(
            jax.ShapeDtypeStruct((ORB, 6, 32, 128), F32),
            jax.ShapeDtypeStruct((8, 128), F32),
        ),
        in_specs=[vmem] * 6 + [anywhere],
        out_specs=(anywhere, vmem),
        scratch_shapes=[
            pltpu.VMEM((2 * PAIRS, 512, WIDE), F8),
            pltpu.VMEM((2 * PAIRS, 1, WIDE), I32),
            pltpu.VMEM((2 * PAIRS, 8, WIDE), F32),
            pltpu.VMEM((2 * ORB * STRIP, 512), F8),
            pltpu.VMEM((2, ORB, 6, 32, 128), BF16),
            pltpu.VMEM((2, ORB, 6, 32, 128), BF16),
            pltpu.VMEM((2, ORB, 6, 32, 128), BF16),
            pltpu.VMEM((2, 2, ORB * 8, 128), F32),
            pltpu.VMEM((2, 2, ORB * 8, 128), F32),
            pltpu.VMEM((2, ORB * 8, 128), F32),
            pltpu.VMEM((2, 128, 128), BF16),
            pltpu.VMEM((2, 8, 128), I32),
            pltpu.VMEM((2, 8, 128), F32),
            pltpu.VMEM((ORB, 6, 32, 128), F32),
            pltpu.VMEM((ORB, 6, 32, 128), F32),
            pltpu.VMEM((2, ORB * STRIP, 512), F32),
            pltpu.VMEM((ORB, ROWS, 128), F32),
            pltpu.VMEM((PANEL_DEV, 6, 32, 128), BF16),
            pltpu.VMEM((ROWS, PANEL_DEV, 128), BF16),
            pltpu.VMEM((CHUNK, PEERS * PANEL_DEV, 128), BF16),
            pltpu.VMEM((PEERS, ORB * CHUNK, 128), BF16),
            pltpu.VMEM((PEERS, ORB * CHUNK, 128), BF16),
            pltpu.VMEM((PEERS * ORB * CHUNK, 128), F32),
            pltpu.VMEM((4, ORB * PEERS, 128), F32),
            pltpu.VMEM((PEERS, 2 * ORB, 256), F32),
            pltpu.VMEM((PEERS, 2 * ORB, 256), F32),
            pltpu.VMEM((2 * ORB, 256), F32),
            pltpu.VMEM((PEERS, 8, 128), F32),
            pltpu.VMEM((PEERS, 8, 128), F32),
            dma((2, 2)), dma((2, 2)),
            dma((2, 2)), dma((2, 2)),
            dma((PEERS,)), dma((PEERS,)), dma,
            dma((PEERS,)), dma((PEERS,)),
            dma((PEERS,)), dma((PEERS,)),
            dma((PEERS,)), dma((PEERS,)),
            dma,
        ],
        compiler_params=pltpu.CompilerParams(
            collective_id=0, has_side_effects=True, vmem_limit_bytes=60 * 2**20
        ),
    )(
        orbitals,
        potential,
        support,
        projectors,
        slot_rows,
        energies.transpose(0, 2, 1),
        panel_orbitals,
    )
    return pl.pallas_call(
        finish,
        out_shape=(
            jax.ShapeDtypeStruct((ORB, 6, 32, 128), F32),
            jax.ShapeDtypeStruct((ORB, PANEL_DEV), F32),
        ),
        in_specs=[vmem] * 2,
        out_specs=(vmem, vmem),
    )(raw, sums)


def solution(mesh):
    return jax.shard_map(
        per_device,
        mesh=mesh,
        in_specs=(
            P("band", "dom", None, None),
            P("dom", None, None),
            P("dom", None, None, None),
            P("dom", None, None, None, None),
            P("dom", None, None),
            P(),
            P("band", "dom", None, None),
        ),
        out_specs=(P("band", "dom", None, None), P("dom", "band")),
        check_vma=False,
    )
```
